256 devices in a mesh: lon: 16 (over y_hi, z), lat: 4 (over x), head: 4 (over y_lo, core).
Axes of the slice: x: 4, y: 4 (y_hi: 2, y_lo: 2; y = y_hi * 2 + y_lo), z: 8, core: 2. Of those that a mesh axis runs over, the one named last changes fastest.
Arguments:
- tokens: bfloat16 [2, 24, 384, 1024], P(None, 'lat', 'lon'), may hold values from -6 to 6
- norm_gain: float32 [1024], replicated, may hold values from 0.5 to 1.5
- w_qkv: bfloat16 [1024, 3072], P(None, 'head'), may hold values from -0.1875 to 0.1875
- w_out: bfloat16 [1024, 1024], P('head'), may hold values from -0.1875 to 0.1875
- bias_table: float32 [759, 16], P(None, 'head'), may hold values from -3 to 300
- cotangent: bfloat16 [2, 24, 384, 1024], P(None, 'lat', 'lon'), may hold values from -6 to 6
Outputs:
- layer_out: bfloat16 [2, 24, 384, 1024], P(None, 'lat', 'lon')
- grad_tokens: bfloat16 [2, 24, 384, 1024], P(None, 'lat', 'lon')
- grad_qkv: float32 [1024, 3072], P(('lon', 'lat'), 'head')
- grad_out: float32 [1024, 1024], P('head', ('lon', 'lat'))
The draws below stay inside these ranges and needn't reach their ends.
All inputs are finite; a program needn't handle non-finite values.
Results may differ from the reference program's by a relative error of at most 0.013.
Values may be sent and summed in bfloat16 or wider, within the bound.
A program may use at most 64 MiB of HBM per device.

```python
import jax
import jax.numpy as jnp
from jax import lax

D = 1024
HEADS = 16
HEAD_DIM = 64
LEV = 2
WLAT = 6
WLON = 12
NLAT = 24
NLON = 384
NREL = 759
N_HEAD = 4


def draw_bias_table(key, part):
    key = jax.random.fold_in(key, 7)
    table_shape = (NREL, HEADS)
    values = jnp.clip(jax.random.normal(key, table_shape, jnp.float32), -3.0, 3.0)
    return values


def strengthened(values, rng, source, target, parts, factor):
    def block_of(position):
        return (jnp.arange(values.shape[position]) // (values.shape[position] // parts)).reshape((-1,) + (1,) * (values.ndim - 1 - position))

    first = jax.random.permutation(rng, parts)[block_of(target)]
    far = (block_of(target) + parts // 2) % parts
    return jnp.where((block_of(source) == first) | (block_of(source) == far), factor * values, values)


def block_levels(key, extent, cuts, smallest, largest):
    level = 1.0
    for dim, parts in cuts:
        steps = jax.random.uniform(jax.random.fold_in(jax.random.fold_in(key, 6), dim), (parts,), jnp.float32, smallest / len(cuts), largest / len(cuts))
        level = level * jnp.repeat(jnp.exp(steps), extent[dim] // parts).reshape((-1,) + (1,) * (len(extent) - 1 - dim))
    return level


def gaussian(key, shape, spread, limit, shards=(), kind=jnp.bfloat16):
    drawn = spread * jax.random.normal(key, shape, jnp.float32)
    if shards:
        drawn = drawn * block_levels(key, shape, shards, -0.22, 0.18)
    return jnp.clip(drawn, -limit, limit).astype(kind)


def noise_with(own_key, extent, spread, limit, pieces, heavy, held_as=jnp.bfloat16):
    array = spread * jax.random.normal(own_key, extent, jnp.float32)
    if pieces:
        array = array * block_levels(own_key, extent, pieces, -0.22, 0.18)
    return jnp.clip(strengthened(array, jax.random.fold_in(own_key, 3), *heavy), -limit, limit).astype(held_as)


def setup_inputs(seed: int = 0) -> dict:
    streams_of = jax.random.split(jax.random.key(seed), 7)
    tokens = gaussian(streams_of[0], (LEV, NLAT, NLON, D), 1.0, 6.0, ((1, 4), (2, 16)))
    norm_gain = jnp.clip(1.0 + 0.1 * jax.random.normal(streams_of[1], (D,), jnp.float32), 0.5, 1.5)
    w_qkv = gaussian(streams_of[2], (D, 3 * D), D ** -0.5, 0.1875, ((1, 4),))
    w_out = gaussian(streams_of[3], (D, D), D ** -0.5, 0.1875, ((0, 4),))
    bias_table = draw_bias_table(jax.random.fold_in(streams_of[6], 71), 0)
    cotangent = noise_with(streams_of[5], (LEV, NLAT, NLON, D), 1.0, 6.0, ((1, 4), (2, 16)), (2, 3, 16, 2.0))
    return {"tokens": tokens, "norm_gain": norm_gain, "w_qkv": w_qkv, "w_out": w_out, "bias_table": bias_table, "cotangent": cotangent}


EPSILON = 1e-05
NEG_FILL = -1e+30

def normalize(values, norm_gain):
    floats = values.astype(jnp.float32)
    center = floats - lax.optimization_barrier(jnp.mean(floats, axis=-1, keepdims=True))
    inverse = lax.rsqrt(lax.optimization_barrier(jnp.mean(center * center, axis=-1, keepdims=True)) + EPSILON)
    scaled = center * inverse
    return ((scaled * norm_gain).astype(jnp.bfloat16), scaled, inverse)

def relative_index():
    window_size = LEV * WLAT * WLON
    cell_idx = jnp.arange(window_size, dtype=jnp.int32)
    level_pos = cell_idx // (WLAT * WLON)
    lat_pos = cell_idx // WLON % WLAT
    lon_pos = cell_idx % WLON
    span_lat = 2 * WLAT - 1
    span_lon = 2 * WLON - 1
    return ((level_pos[:, None] - level_pos[None, :] + LEV - 1) * span_lat * span_lon + (lat_pos[:, None] - lat_pos[None, :] + WLAT - 1) * span_lon + lon_pos[:, None] - lon_pos[None, :] + WLON - 1).astype(jnp.int32)

def to_windows(field):
    level_count, lat_count, lon_count, channels = field.shape
    split = field.reshape(level_count, lat_count // WLAT, WLAT, lon_count // WLON, WLON, channels)
    return split.transpose(1, 3, 0, 2, 4, 5).reshape(lat_count // WLAT, lon_count // WLON, level_count * WLAT * WLON, channels)

def from_windows(blocks, level_count):
    lat_blocks, lon_blocks, window_size, channels = blocks.shape
    split = blocks.reshape(lat_blocks, lon_blocks, level_count, WLAT, WLON, channels)
    return split.transpose(2, 0, 3, 1, 4, 5).reshape(level_count, lat_blocks * WLAT, lon_blocks * WLON, channels)

def attend(query_part, key_part, value_part, grad_part, rel_bias, allowed):
    scale = HEAD_DIM ** (-0.5)
    query_f = query_part.astype(jnp.float32)
    key_f = key_part.astype(jnp.float32)
    value_f = value_part.astype(jnp.float32)
    grad_f = grad_part.astype(jnp.float32)
    scores = jnp.einsum('wqhe,wkhe->whqk', query_f, key_f) * scale + rel_bias[None]
    scores = jnp.where(allowed[:, None], scores, NEG_FILL)
    peak = lax.optimization_barrier(jnp.max(scores, axis=-1, keepdims=True))
    raised = jnp.exp(scores - peak)
    prob_full = raised / lax.optimization_barrier(jnp.sum(raised, axis=-1, keepdims=True))
    prob_half = prob_full.astype(jnp.bfloat16)
    prob_back = prob_half.astype(jnp.float32)
    attended = jnp.einsum('whqk,wkhe->wqhe', prob_back, value_f).astype(jnp.bfloat16)
    grad_prob = jnp.einsum('wqhe,wkhe->whqk', grad_f, value_f)
    row_term = lax.optimization_barrier(jnp.sum(prob_full * grad_prob, axis=-1, keepdims=True))
    grad_score = (prob_full * (grad_prob - row_term) * scale).astype(jnp.bfloat16).astype(jnp.float32)
    grad_query = jnp.einsum('whqk,wkhe->wqhe', grad_score, key_f)
    grad_key = jnp.einsum('whqk,wqhe->wkhe', grad_score, query_f)
    grad_value = jnp.einsum('whqk,wqhe->wkhe', prob_back, grad_f)
    return (attended, jnp.stack([grad_query, grad_key, grad_value], axis=3).astype(jnp.bfloat16))

def rounded(values):
    return lax.optimization_barrier(values.astype(jnp.bfloat16)).astype(jnp.float32)

def reference(tokens, norm_gain, w_qkv, w_out, bias_table, cotangent):
    cells = LEV * NLAT * NLON
    shift_lat = WLAT // 2
    shift_lon = WLON // 2
    window_size = LEV * WLAT * WLON
    flat_tokens = tokens.reshape(cells, D)
    flat_grad = cotangent.reshape(cells, D)
    normed, scaled, inverse = normalize(flat_tokens, norm_gain)
    projected = jnp.dot(normed, w_qkv, preferred_element_type=jnp.float32).astype(jnp.bfloat16)
    d_attended = jnp.dot(flat_grad, w_out.T, preferred_element_type=jnp.float32).astype(jnp.bfloat16)
    joined = jnp.concatenate([projected, d_attended], axis=1).reshape(LEV, NLAT, NLON, 4 * D)
    rolled = jnp.roll(joined, (-shift_lat, -shift_lon), axis=(1, 2))
    blocks = to_windows(rolled)
    rel_bias = jnp.transpose(bias_table[relative_index()], (2, 0, 1))
    lat_pos = jnp.arange(window_size, dtype=jnp.int32) // WLON % WLAT

    def one_row(inputs):
        row_idx, row_blocks = inputs
        initial = (row_idx * WLAT + lat_pos + shift_lat) % NLAT
        allowed = jnp.abs(initial[:, None] - initial[None, :]) < WLAT
        lon_count = row_blocks.shape[0]
        qkv_part = row_blocks[:, :, :3 * D].reshape(lon_count, window_size, HEADS, 3, HEAD_DIM)
        grad_part = row_blocks[:, :, 3 * D:].reshape(lon_count, window_size, HEADS, HEAD_DIM)
        attended, dstack = attend(qkv_part[:, :, :, 0], qkv_part[:, :, :, 1], qkv_part[:, :, :, 2], grad_part, rel_bias, allowed[None])
        return jnp.concatenate([attended.reshape(lon_count, window_size, D), dstack.reshape(lon_count, window_size, 3 * D)], axis=2)
    results = lax.map(one_row, (jnp.arange(NLAT // WLAT, dtype=jnp.int32), blocks))
    restored = jnp.roll(from_windows(results, LEV), (shift_lat, shift_lon), axis=(1, 2)).reshape(cells, 4 * D)
    attended = restored[:, :D]
    dqkv = restored[:, D:]
    group_width = D // N_HEAD
    attn_total = jnp.zeros((cells, D), jnp.float32)
    dnormed = jnp.zeros((cells, D), jnp.float32)
    for group_idx in range(N_HEAD):
        first_col = group_idx * group_width
        out_term = jnp.dot(attended[:, first_col:first_col + group_width], w_out[first_col:first_col + group_width], preferred_element_type=jnp.float32)
        attn_total = attn_total + rounded(out_term)
        wide_first = 3 * first_col
        in_term = jnp.dot(dqkv[:, wide_first:wide_first + 3 * group_width], w_qkv[:, wide_first:wide_first + 3 * group_width].T, preferred_element_type=jnp.float32)
        dnormed = dnormed + rounded(in_term)
    layer_out = (flat_tokens.astype(jnp.float32) + attn_total).astype(jnp.bfloat16)
    grad_qkv = jnp.dot(normed.T, dqkv, preferred_element_type=jnp.float32)
    grad_out = jnp.dot(attended.T, flat_grad, preferred_element_type=jnp.float32)
    scaled_grad = dnormed * norm_gain
    mean_grad = lax.optimization_barrier(jnp.mean(scaled_grad, axis=-1, keepdims=True))
    mean_mixed = lax.optimization_barrier(jnp.mean(scaled_grad * scaled, axis=-1, keepdims=True))
    grad_tokens = (flat_grad.astype(jnp.float32) + (scaled_grad - mean_grad - scaled * mean_mixed) * inverse).astype(jnp.bfloat16)
    return (layer_out.reshape(LEV, NLAT, NLON, D), grad_tokens.reshape(LEV, NLAT, NLON, D), grad_qkv, grad_out)
```

```python
import functools

import jax
import jax.numpy as jnp
import ml_dtypes
import numpy as np
from jax import lax
from jax.experimental import pallas as pl
from jax.experimental.pallas import tpu as pltpu
from jax.sharding import PartitionSpec as P

MESH = pl.DeviceIdType.MESH
HEAD_DIM = 64
LEV = 2
WLAT = 6
WLON = 12
LON = 24
WINDOW = LEV * WLAT * WLON
CELLS = LEV * WLAT * LON
EPSILON = 1e-05
NEG_FILL = -1e30
F32 = jnp.float32
BF16 = jnp.bfloat16

G_START = (0, 112, 224, 272)
G_ROWS = 320
U_START = (0, 64, 128, 160)
U_ROWS = 192
SEL = 384


def quarter(row, col):
    down, right = row >= 3, col >= 18
    part = (2 if right else 0) + (1 if down else 0)
    width = 6 if right else 18
    return part, (row % 3) * width + (col - 18 if right else col), 3 * width


def tables():
    own = np.zeros((G_ROWS, CELLS), np.float32)
    compact = np.zeros((CELLS, G_ROWS), np.float32)
    level = np.zeros((LEV, CELLS // LEV, CELLS), np.float32)
    spread = np.zeros((U_ROWS, CELLS // LEV), np.float32)
    natural = np.zeros((CELLS // LEV, U_ROWS), np.float32)
    t_start = (0, 54, 108, 126)
    for lv in range(LEV):
        for row in range(WLAT):
            for col in range(LON):
                part, index, size = quarter(row, col)
                held = G_START[part] + lv * size + index
                src_row = row + 3 if row < 3 else row - 3
                src_col = col + 6 if col < 18 else col - 18
                own[held, lv * 144 + src_row * LON + src_col] = 1
                place = (col // WLON) * WINDOW + lv * 72 + row * WLON + col % WLON
                compact[place, held] = 1
                level[lv, t_start[part] + index, place] = 1
                if lv == 0:
                    spread[U_START[part] + index, t_start[part] + index] = 1
                    natural[src_row * LON + src_col, U_START[part] + index] = 1
    select = np.zeros((SEL, WINDOW), np.float32)
    for i in range(WINDOW):
        select[(i // 72) * 253 + (i // WLON % WLAT) * 23 + i % WLON, i] = 1
    half = np.arange(WINDOW) // WLON % WLAT >= 3
    cross = (half[:, None] != half[None, :]).astype(np.float32)
    exact = [t.astype(ml_dtypes.bfloat16) for t in (own, compact, level, spread, natural, select, np.eye(128, dtype=np.float32))]
    return exact + [cross]


def dot(a, b, ca=1, cb=0):
    return lax.dot_general(a, b, (((ca,), (cb,)), ((), ())), preferred_element_type=F32)


def layer_norm(floats):
    center = floats - jnp.mean(floats, axis=-1, keepdims=True)
    inverse = lax.rsqrt(jnp.mean(center * center, axis=-1, keepdims=True) + EPSILON)
    return center * inverse, inverse


def kernel(
    nlon, nlat,
    tok_ref, cot_ref, gain_ref, wqkv_ref, wout_ref, table_ref,
    own_ref, compact_ref, level_ref, spread_ref, natural_ref, select_ref, eye_ref, cross_ref,
    layer_ref, dtok_ref, gqkv_ref, gout_ref,
    sent, held, tokc, cotc, normed, normed_t, cot_t, qkv, datt, rolled, bias, dqkv, att,
    wgt, from_x, sum_x, from_z, sum_z, from_y,
    term, from_core, to_side, from_side, result, spread_out, back, final,
    send_sem, recv_sem, out_sem,
):
    lon, lat, head = lax.axis_index("lon"), lax.axis_index("lat"), lax.axis_index("head")
    nz = nlon // 2
    y_hi, z = lon // nz, lon % nz
    kind, core = head // 2, head % 2
    lat_up, lat_down = (lat + 1) % nlat, (lat + nlat - 1) % nlat
    lon_up, lon_down = (lon + 1) % nlon, (lon + nlon - 1) % nlon
    sibling = {"head": kind * 2 + 1 - core}
    side = {"head": (1 - kind) * 2 + core}
    x_up = [{"lat": (lat + d) % nlat} for d in range(1, nlat)]
    x_down = [{"lat": (lat + nlat - d) % nlat} for d in range(1, nlat)]
    z_up = [{"lon": y_hi * nz + (z + d) % nz} for d in range(1, nz)]
    z_down = [{"lon": y_hi * nz + (z + nz - d) % nz} for d in range(1, nz)]
    far = {"lon": (1 - y_hi) * nz + z}

    sources = x_down + z_down + [
        far, sibling, side,
        {"lon": lon_up}, {"lon": lon_down},
        {"lat": lat_up, "lon": lon_up}, {"lat": lat_down, "lon": lon_down},
    ]
    barrier = pltpu.get_barrier_semaphore()
    for source in sources:
        pl.semaphore_signal(barrier, inc=1, device_id=source, device_id_type=MESH)

    count = [0]

    def remote(src, dst, target):
        index = count[0]
        count[0] += 1
        return pltpu.make_async_remote_copy(
            src_ref=src, dst_ref=dst, send_sem=send_sem.at[index], recv_sem=recv_sem.at[index],
            device_id=target, device_id_type=MESH,
        )

    started = []

    def start(copies):
        for copy in copies:
            copy.start()
        started.extend(copies)
        return copies

    for i, ref in enumerate((tok_ref, cot_ref)):
        arranged = dot(own_ref[...], ref[...]).astype(BF16)
        held[i, 0:112] = arranged[0:112]
        sent[i] = arranged[112:]
    pl.semaphore_wait(barrier, len(sources))
    parts = [(112, 112, {"lat": lat_down}), (224, 48, {"lon": lon_down}), (272, 48, {"lat": lat_down, "lon": lon_down})]
    shifted = start([
        remote(sent.at[core, pl.ds(at - 112, size)], held.at[core, pl.ds(at, size)], target) for at, size, target in parts
    ])

    for h in range(4):
        stepped = jnp.broadcast_to(table_ref[h : h + 1, :], (16, table_ref.shape[1]))
        stepped = pltpu.roll(stepped, 0, 1, stride=1, stride_axis=0)
        for step in range(LEV * WLAT):
            offset = (step // WLAT) * 253 + (step % WLAT) * 23
            shift = (offset - 379) % table_ref.shape[1]
            moved = pltpu.roll(stepped, shift, 1)
            rolled[WLON * step : WLON * step + WLON, :] = moved[0:WLON, 0:SEL]
        rest = rolled[...]
        total = jnp.zeros((WINDOW, WINDOW), F32)
        for _ in range(3):
            piece = rest.astype(BF16)
            rest = rest - piece.astype(F32)
            total = total + dot(piece, select_ref[...])
        excluded = (cross_ref[...] > 0.5) & (lat == nlat - 1)
        bias[h] = jnp.where(excluded, NEG_FILL, total)

    forwards = []
    for copy, (at, size, _) in zip(shifted, parts):
        copy.wait_recv()
        forwards += start([remote(held.at[core, pl.ds(at, size)], held.at[core, pl.ds(at, size)], sibling)])
    for copy in forwards:
        copy.wait_recv()

    tokc[...] = dot(compact_ref[...], held[0]).astype(BF16)
    cotc[...] = dot(compact_ref[...], held[1]).astype(BF16)
    for at in range(0, CELLS, 48):
        scaled, _ = layer_norm(tokc[at : at + 48, :].astype(F32))
        normed[at : at + 48, :] = (scaled * gain_ref[...]).astype(BF16)
    qkv[...] = dot(normed[...], wqkv_ref[...]).astype(BF16)
    datt[...] = dot(cotc[...], wout_ref[...], 1, 1).astype(BF16)
    for at in range(0, normed.shape[1], 128):
        normed_t[at : at + 128, :] = dot(eye_ref[...], normed[:, at : at + 128], 1, 1).astype(BF16)
        cot_t[at : at + 128, :] = dot(eye_ref[...], cotc[:, at : at + 128], 1, 1).astype(BF16)

    def attend(w, h):
        rows = pl.ds(w * WINDOW, WINDOW)
        first = 3 * HEAD_DIM * h
        query = qkv[rows, first : first + 64]
        key = qkv[rows, first + 64 : first + 128]
        value = qkv[rows, first + 128 : first + 192]
        grad = datt[rows, 64 * h : 64 * h + 64]
        scores = dot(key, query, 1, 1) * (HEAD_DIM ** -0.5) + bias[h]
        raised = jnp.exp(scores - jnp.max(scores, axis=0, keepdims=True))
        prob = raised * (1.0 / jnp.sum(raised, axis=0, keepdims=True))
        half = prob.astype(BF16)
        grad_prob = dot(value, grad, 1, 1)
        row_term = jnp.sum(prob * grad_prob, axis=0, keepdims=True)
        grad_score = (prob * (grad_prob - row_term) * (HEAD_DIM ** -0.5)).astype(BF16)
        att[rows, 64 * h : 64 * h + 64] = dot(half, value, 0, 0).astype(BF16)
        dqkv[rows, first : first + 64] = dot(grad_score, key, 0, 0).astype(BF16)
        dqkv[rows, first + 64 : first + 128] = dot(grad_score, query, 1, 0).astype(BF16)
        dqkv[rows, first + 128 : first + 192] = dot(half, grad, 1, 0).astype(BF16)

    rows_out = wgt.shape[3]
    on_x, on_z, on_y = [], [], []
    for pair in range(2):
        for h in (2 * pair, 2 * pair + 1):
            for w in range(2):
                attend(w, h)
        wide = dot(normed_t[...], dqkv[:, 384 * pair : 384 * pair + 384]).astype(BF16)
        wgt[pair, :, :, :, 0:384] = wide.reshape(nlon, nlat, rows_out, 384)
        narrow = dot(cot_t[...], att[:, 128 * pair : 128 * pair + 128]).astype(BF16)
        wgt[pair, :, :, :, 384:512] = narrow.reshape(nlon, nlat, rows_out, 128)
        on_x.append(start([
            remote(wgt.at[pair, :, target["lat"]], from_x.at[pair, d], target) for d, target in enumerate(x_up)
        ]))

    for lv in (1 - core, core):
        order = level_ref[lv]
        att_l = dot(order, att[...]).astype(BF16)
        dqkv_l = dot(order, dqkv[...]).astype(BF16)
        term[lv, 0] = dot(att_l, wout_ref[...]).astype(BF16)
        term[lv, 1] = dot(dqkv_l, wqkv_ref[...], 1, 1).astype(BF16)
        if lv is not core:
            on_core = start([remote(term.at[1 - core], from_core, sibling)])[0]
    tok_l = dot(level_ref[core], tokc[...])
    cot_l = dot(level_ref[core], cotc[...])

    def pass_x(pair):
        for copy in on_x[pair]:
            copy.wait_recv()
        total = wgt[pair, :, lat].astype(F32)
        for d in range(nlat - 1):
            total = total + from_x[pair, d].astype(F32)
        sum_x[pair] = total.astype(BF16).reshape(sum_x.shape[1:])
        on_z.append(start([
            remote(sum_x.at[pair, :, target["lon"] - y_hi * nz], from_z.at[pair, d], target) for d, target in enumerate(z_up)
        ]))

    def pass_z(pair):
        for copy in on_z[pair]:
            copy.wait_recv()
        total = sum_x[pair, :, z].astype(F32)
        for d in range(nz - 1):
            total = total + from_z[pair, d].astype(F32)
        sum_z[pair] = total.astype(BF16)
        on_y.append(start([remote(sum_z.at[pair, 1 - y_hi], from_y.at[pair], far)])[0])

    def pass_y(pair):
        on_y[pair].wait_recv()
        total = sum_z[pair, y_hi].astype(F32) + from_y[pair].astype(F32)
        gqkv_ref[:, 384 * pair : 384 * pair + 384] = total[:, 0:384]
        gout_ref[:, 128 * pair : 128 * pair + 128] = total[:, 384:512]

    on_core.wait_recv()
    to_side[...] = (term[core, 1 - kind].astype(F32) + from_core[1 - kind].astype(F32)).astype(BF16)
    on_side = start([remote(to_side, from_side, side)])[0]
    pass_x(0)
    on_side.wait_recv()
    total = term[core, kind].astype(F32) + from_core[kind].astype(F32) + from_side[...].astype(F32)

    @pl.when(kind == 0)
    def _():
        result[...] = (tok_l + total).astype(BF16)

    @pl.when(kind == 1)
    def _():
        scaled, inverse = layer_norm(tok_l)
        grad = total * gain_ref[...]
        mean_grad = jnp.mean(grad, axis=-1, keepdims=True)
        mean_mixed = jnp.mean(grad * scaled, axis=-1, keepdims=True)
        result[...] = (cot_l + (grad - mean_grad - scaled * mean_mixed) * inverse).astype(BF16)

    spread_out[...] = dot(spread_ref[...], result[...]).astype(BF16)
    back[0:64] = spread_out[0:64]
    returned = start([
        remote(spread_out.at[pl.ds(at, size)], back.at[pl.ds(at, size)], target)
        for at, size, target in ((64, 64, {"lat": lat_up}), (128, 32, {"lon": lon_up}), (160, 32, {"lat": lat_up, "lon": lon_up}))
    ])
    pass_x(1)
    pass_z(0)
    for copy in returned:
        copy.wait_recv()
    final[kind, core] = dot(natural_ref[...], back[...]).astype(BF16)
    own_side, own_core = start([
        remote(final.at[kind, core], final.at[kind, core], side),
        remote(final.at[kind, core], final.at[kind, core], sibling),
    ])
    pass_z(1)
    pass_y(0)
    own_side.wait_recv()
    other_core = start([remote(final.at[1 - kind, core], final.at[1 - kind, core], sibling)])[0]
    pass_y(1)
    own_core.wait_recv()
    other_core.wait_recv()
    outs = [
        pltpu.make_async_copy(final.at[0], layer_ref, out_sem.at[0]),
        pltpu.make_async_copy(final.at[1], dtok_ref, out_sem.at[1]),
    ]
    for copy in outs:
        copy.start()
    for copy in started:
        copy.wait_send()
    for copy in outs:
        copy.wait()


def body(tokens, norm_gain, w_qkv, w_out, bias_table, cotangent):
    nlon, nlat = lax.axis_size("lon"), lax.axis_size("lat")
    nz = nlon // 2
    width = tokens.shape[-1]
    rows = width // (nlon * nlat)
    table = jnp.pad(bias_table.T, ((0, 4), (0, 768 - bias_table.shape[0])))
    vmem = pl.BlockSpec(memory_space=pltpu.VMEM)
    hbm = pl.BlockSpec(memory_space=pl.ANY)
    copies = 3 + 3 + 2 * (nlat - 1) + 2 * (nz - 1) + 2 + 2 + 3 + 3
    shape = lambda *dims: pltpu.VMEM(dims, BF16)
    layer, dtok, gqkv, gout = pl.pallas_call(
        functools.partial(kernel, nlon, nlat),
        out_shape=(
            jax.ShapeDtypeStruct((LEV, CELLS // LEV, width), BF16),
            jax.ShapeDtypeStruct((LEV, CELLS // LEV, width), BF16),
            jax.ShapeDtypeStruct((rows, 768), F32),
            jax.ShapeDtypeStruct((rows, 256), F32),
        ),
        in_specs=[vmem] * 14,
        out_specs=(hbm, hbm, vmem, vmem),
        scratch_shapes=[
            shape(2, G_ROWS - 112, width),
            shape(2, G_ROWS, width),
            shape(CELLS, width),
            shape(CELLS, width),
            shape(CELLS, width),
            shape(width, CELLS),
            shape(width, CELLS),
            shape(CELLS, 768),
            shape(CELLS, 256),
            pltpu.VMEM((WINDOW, SEL), F32),
            pltpu.VMEM((4, WINDOW, WINDOW), F32),
            shape(CELLS, 768),
            shape(CELLS, 256),
            shape(2, nlon, nlat, rows, 512),
            shape(2, nlat - 1, nlon, rows, 512),
            shape(2, 2, nz, rows, 512),
            shape(2, max(nz - 1, 1), 2, rows, 512),
            shape(2, 2, rows, 512),
            shape(2, rows, 512),
            shape(LEV, 2, CELLS // LEV, width),
            shape(2, CELLS // LEV, width),
            shape(CELLS // LEV, width),
            shape(CELLS // LEV, width),
            shape(CELLS // LEV, width),
            shape(U_ROWS, width),
            shape(U_ROWS, width),
            shape(2, LEV, CELLS // LEV, width),
            pltpu.SemaphoreType.DMA((copies,)),
            pltpu.SemaphoreType.DMA((copies,)),
            pltpu.SemaphoreType.DMA((2,)),
        ],
        compiler_params=pltpu.CompilerParams(
            collective_id=0, has_side_effects=True, vmem_limit_bytes=56 * 1024 * 1024
        ),
    )(
        tokens.reshape(CELLS, width), cotangent.reshape(CELLS, width), norm_gain.reshape(1, width),
        w_qkv, w_out, table, *[jnp.asarray(t) for t in tables()],
    )
    field = (LEV, WLAT, LON, width)
    return layer.reshape(field), dtok.reshape(field), gqkv, gout.T


def solution(mesh):
    in_specs = (
        P(None, "lat", "lon", None),
        P(),
        P(None, "head"),
        P("head", None),
        P(None, "head"),
        P(None, "lat", "lon", None),
    )
    out_specs = (
        P(None, "lat", "lon", None),
        P(None, "lat", "lon", None),
        P(("lon", "lat"), "head"),
        P("head", ("lon", "lat")),
    )
    return jax.shard_map(body, mesh=mesh, in_specs=in_specs, out_specs=out_specs, check_vma=False)
```

```python
import functools

import jax
import jax.numpy as jnp
import ml_dtypes
import numpy as np
from jax import lax
from jax.experimental import pallas as pl
from jax.experimental.pallas import tpu as pltpu
from jax.sharding import PartitionSpec as P

MESH = pl.DeviceIdType.MESH
HEAD_DIM = 64
LEV = 2
WLAT = 6
WLON = 12
LON = 24
WINDOW = LEV * WLAT * WLON
CELLS = LEV * WLAT * LON
EPSILON = 1e-05
NEG_FILL = -1e30
F32 = jnp.float32
BF16 = jnp.bfloat16

G_START = (0, 112, 224, 272)
G_ROWS = 320
T_START = (96, 0, 54, 72)
T_AWAY = 96
T_ROWS = 160
U_START = (None, 0, 64, 96)
U_ROWS = 128
SEL = 384


def quarter(row, col):
    down, right = row >= 3, col >= 18
    part = (2 if right else 0) + (1 if down else 0)
    width = 6 if right else 18
    return part, (row % 3) * width + (col - 18 if right else col), 3 * width


def tables():
    own = np.zeros((G_ROWS, CELLS), np.float32)
    compact = np.zeros((CELLS, G_ROWS), np.float32)
    level = np.zeros((LEV, T_ROWS, CELLS), np.float32)
    spread = np.zeros((U_ROWS, T_AWAY), np.float32)
    natural = np.zeros((CELLS // LEV, T_ROWS), np.float32)
    for lv in range(LEV):
        for row in range(WLAT):
            for col in range(LON):
                part, index, size = quarter(row, col)
                held = G_START[part] + lv * size + index
                src_row = row + 3 if row < 3 else row - 3
                src_col = col + 6 if col < 18 else col - 18
                own[held, lv * 144 + src_row * LON + src_col] = 1
                place = (col // WLON) * WINDOW + lv * 72 + row * WLON + col % WLON
                compact[place, held] = 1
                level[lv, T_START[part] + index, place] = 1
                if lv == 0:
                    natural[src_row * LON + src_col, T_START[part] + index] = 1
                    if part:
                        spread[U_START[part] + index, T_START[part] + index] = 1
    select = np.zeros((SEL, WINDOW), np.float32)
    for i in range(WINDOW):
        select[(i // 72) * 253 + (i // WLON % WLAT) * 23 + i % WLON, i] = 1
    half = np.arange(WINDOW) // WLON % WLAT >= 3
    cross = (half[:, None] != half[None, :]).astype(np.float32)
    exact = [t.astype(ml_dtypes.bfloat16) for t in (own, compact, level, spread, spread.T, natural, select, np.eye(128, dtype=np.float32))]
    return exact + [cross]


def dot(a, b, ca=1, cb=0):
    return lax.dot_general(a, b, (((ca,), (cb,)), ((), ())), preferred_element_type=F32)


def layer_norm(floats):
    center = floats - jnp.mean(floats, axis=-1, keepdims=True)
    inverse = lax.rsqrt(jnp.mean(center * center, axis=-1, keepdims=True) + EPSILON)
    return center * inverse, inverse


def kernel(
    nlon, nlat,
    tok_ref, cot_ref, gain_ref, wqkv_ref, wout_ref, table_ref,
    own_ref, compact_ref, level_ref, spread_ref, gather_ref, natural_ref, select_ref, eye_ref, cross_ref,
    layer_ref, dtok_ref, gqkv_ref, gout_ref,
    sent, held, tokc, cotc, normed, normed_t, cot_t, qkv, datt, wide_table, rolled, bias, dqkv, att,
    wgt, near_x, sum_x, near_z, first_z, sum_z, last_x, sum_y, from_y,
    term, from_core, to_side, from_side, result, spread_out, back, final, fields,
    send_sem, recv_sem, out_sem,
):
    lon, lat, head = lax.axis_index("lon"), lax.axis_index("lat"), lax.axis_index("head")
    nz = nlon // 2
    y_hi, z = lon // nz, lon % nz
    kind, core = head // 2, head % 2
    lat_up, lat_down = (lat + 1) % nlat, (lat + nlat - 1) % nlat
    lon_up, lon_down = (lon + 1) % nlon, (lon + nlon - 1) % nlon
    sibling = {"head": kind * 2 + 1 - core}
    side = {"head": (1 - kind) * 2 + core}
    x_up = [{"lat": (lat + d) % nlat} for d in range(1, nlat)]
    x_down = [{"lat": (lat + nlat - d) % nlat} for d in range(1, nlat)]
    z_up = [{"lon": y_hi * nz + (z + d) % nz} for d in range(1, nz)]
    z_down = [{"lon": y_hi * nz + (z + nz - d) % nz} for d in range(1, nz)]
    far = {"lon": (1 - y_hi) * nz + z}

    sources = x_down + z_down + [
        far, sibling, side,
        {"lon": lon_up}, {"lon": lon_down},
        {"lat": lat_up, "lon": lon_up}, {"lat": lat_down, "lon": lon_down},
    ]
    barrier = pltpu.get_barrier_semaphore()
    for source in sources:
        pl.semaphore_signal(barrier, inc=1, device_id=source, device_id_type=MESH)

    count = [0]

    def remote(src, dst, target):
        index = count[0]
        count[0] += 1
        return pltpu.make_async_remote_copy(
            src_ref=src, dst_ref=dst, send_sem=send_sem.at[index], recv_sem=recv_sem.at[index],
            device_id=target, device_id_type=MESH,
        )

    started = []

    def start(copies):
        for copy in copies:
            copy.start()
        started.extend(copies)
        return copies

    for i, ref in enumerate((tok_ref, cot_ref)):
        arranged = dot(own_ref[...], ref[...]).astype(BF16)
        held[i, 0:112] = arranged[0:112]
        sent[i] = arranged[112:]
    pl.semaphore_wait(barrier, len(sources))
    diagonal = {"lat": lat_down, "lon": lon_down}
    parts = [(112, 64, {"lat": lat_down}), (224, 48, {"lon": lon_down}), (272, 48, diagonal), (176, 48, {"lat": lat_down})]
    shifted = start([
        remote(sent.at[core, pl.ds(at - 112, size)], held.at[core, pl.ds(at, size)], target) for at, size, target in parts
    ])

    wide_table[...] = jnp.zeros(wide_table.shape, F32)
    wide_table[0 : table_ref.shape[0], 0:4] = table_ref[...]
    turned = wide_table[...].T
    for h in range(4):
        stepped = jnp.broadcast_to(turned[h : h + 1, :], (16, turned.shape[1]))
        stepped = pltpu.roll(stepped, 0, 1, stride=1, stride_axis=0)
        for step in range(LEV * WLAT):
            offset = (step // WLAT) * 253 + (step % WLAT) * 23
            shift = (offset - 379) % turned.shape[1]
            moved = pltpu.roll(stepped, shift, 1)
            rolled[WLON * step : WLON * step + WLON, :] = moved[0:WLON, 0:SEL]
        rest = rolled[...]
        total = jnp.zeros((WINDOW, WINDOW), F32)
        for _ in range(3):
            piece = rest.astype(BF16)
            rest = rest - piece.astype(F32)
            total = total + dot(piece, select_ref[...])
        excluded = (cross_ref[...] > 0.5) & (lat == nlat - 1)
        bias[h] = jnp.where(excluded, NEG_FILL, total)

    forwards = []
    for copy, (at, size, _) in zip(shifted, parts):
        copy.wait_recv()
        forwards += start([remote(held.at[core, pl.ds(at, size)], held.at[core, pl.ds(at, size)], sibling)])
    for copy in forwards:
        copy.wait_recv()

    tokc[...] = dot(compact_ref[...], held[0]).astype(BF16)
    cotc[...] = dot(compact_ref[...], held[1]).astype(BF16)
    for at in range(0, CELLS, 48):
        scaled, _ = layer_norm(tokc[at : at + 48, :].astype(F32))
        normed[at : at + 48, :] = (scaled * gain_ref[...]).astype(BF16)
    qkv[...] = dot(normed[...], wqkv_ref[...]).astype(BF16)
    datt[...] = dot(cotc[...], wout_ref[...], 1, 1).astype(BF16)
    for at in range(0, normed.shape[1], 128):
        normed_t[at : at + 128, :] = dot(eye_ref[...], normed[:, at : at + 128], 1, 1).astype(BF16)
        cot_t[at : at + 128, :] = dot(eye_ref[...], cotc[:, at : at + 128], 1, 1).astype(BF16)

    def attend(w, h):
        rows = pl.ds(w * WINDOW, WINDOW)
        first = 3 * HEAD_DIM * h
        query = qkv[rows, first : first + 64]
        key = qkv[rows, first + 64 : first + 128]
        value = qkv[rows, first + 128 : first + 192]
        grad = datt[rows, 64 * h : 64 * h + 64]
        scores = dot(key, query, 1, 1) * (HEAD_DIM ** -0.5) + bias[h]
        raised = jnp.exp(scores - jnp.max(scores, axis=0, keepdims=True))
        prob = raised * (1.0 / jnp.sum(raised, axis=0, keepdims=True))
        half = prob.astype(BF16)
        grad_prob = dot(value, grad, 1, 1)
        row_term = jnp.sum(prob * grad_prob, axis=0, keepdims=True)
        grad_score = (prob * (grad_prob - row_term) * (HEAD_DIM ** -0.5)).astype(BF16)
        att[rows, 64 * h : 64 * h + 64] = dot(half, value, 0, 0).astype(BF16)
        dqkv[rows, first : first + 64] = dot(grad_score, key, 0, 0).astype(BF16)
        dqkv[rows, first + 64 : first + 128] = dot(grad_score, query, 1, 0).astype(BF16)
        dqkv[rows, first + 128 : first + 192] = dot(half, grad, 1, 0).astype(BF16)

    rows_out = wgt.shape[4]
    on_first, on_second, on_y = {}, {}, {}

    def weight(h):
        wide = dot(normed_t[...], dqkv[:, 192 * h : 192 * h + 192]).astype(BF16)
        wgt[h, :, :, :, :, 0:192] = wide.reshape(2, nz, nlat, rows_out, 192)
        narrow = dot(cot_t[...], att[:, 64 * h : 64 * h + 64]).astype(BF16)
        wgt[h, :, :, :, :, 192:256] = narrow.reshape(2, nz, nlat, rows_out, 64)
        if h == 0:
            on_first[h] = start([
                remote(wgt.at[h, :, target["lon"] - y_hi * nz], near_z.at[d], target) for d, target in enumerate(z_up)
            ])
        else:
            on_first[h] = start([
                remote(wgt.at[h, :, :, target["lat"]], near_x.at[h - 1, d], target) for d, target in enumerate(x_up)
            ])

    def second(h):
        for copy in on_first[h]:
            copy.wait_recv()
        if h == 0:
            total = wgt[h, :, z].astype(F32)
            for d in range(nz - 1):
                total = total + near_z[d].astype(F32)
            first_z[...] = total.astype(BF16)
            on_second[h] = start([
                remote(first_z.at[:, target["lat"]], last_x.at[d], target) for d, target in enumerate(x_up)
            ])
        else:
            total = wgt[h, :, :, lat].astype(F32)
            for d in range(nlat - 1):
                total = total + near_x[h - 1, d].astype(F32)
            sum_x[h - 1] = total.astype(BF16)
            on_second[h] = start([
                remote(sum_x.at[h - 1, :, target["lon"] - y_hi * nz], sum_z.at[h - 1, d], target) for d, target in enumerate(z_up)
            ])

    def third(h):
        for copy in on_second[h]:
            copy.wait_recv()
        if h == 0:
            total = first_z[:, lat].astype(F32)
            for d in range(nlat - 1):
                total = total + last_x[d].astype(F32)
        else:
            total = sum_x[h - 1, :, z].astype(F32)
            for d in range(nz - 1):
                total = total + sum_z[h - 1, d].astype(F32)
        sum_y[h] = total.astype(BF16)
        on_y[h] = start([remote(sum_y.at[h, 1 - y_hi], from_y.at[h], far)])[0]

    def last(h):
        on_y[h].wait_recv()
        total = sum_y[h, y_hi].astype(F32) + from_y[h].astype(F32)
        gqkv_ref[:, 192 * h : 192 * h + 192] = total[:, 0:192]
        gout_ref[:, 64 * h : 64 * h + 64] = total[:, 192:256]

    for h in range(4):
        for w in range(2):
            attend(w, h)
        if h < 3:
            weight(h)

    chunks = ((0, T_AWAY), (T_AWAY, T_ROWS - T_AWAY))
    on_core = []
    for lv in (1 - core, core):
        for at, size in chunks:
            order = level_ref[lv, at : at + size]
            att_l = dot(order, att[...]).astype(BF16)
            dqkv_l = dot(order, dqkv[...]).astype(BF16)
            term[lv, 0, at : at + size] = dot(att_l, wout_ref[...]).astype(BF16)
            term[lv, 1, at : at + size] = dot(dqkv_l, wqkv_ref[...], 1, 1).astype(BF16)
            if lv is not core:
                on_core += start([
                    remote(term.at[1 - core, :, pl.ds(at, size)], from_core.at[:, pl.ds(at, size)], sibling)
                ])
    on_side = []
    for copy, (at, size) in zip(on_core, chunks):
        copy.wait_recv()
        rows = pl.ds(at, size)
        to_side[rows] = (term[core, 1 - kind, rows].astype(F32) + from_core[1 - kind, rows].astype(F32)).astype(BF16)
        on_side += start([remote(to_side.at[rows], from_side.at[rows], side)])
    weight(3)

    def finish(chunk):
        at, size = chunks[chunk]
        rows = pl.ds(at, size)
        tok_l = dot(level_ref[core, at : at + size], tokc[...])
        cot_l = dot(level_ref[core, at : at + size], cotc[...])
        on_side[chunk].wait_recv()
        total = term[core, kind, rows].astype(F32) + from_core[kind, rows].astype(F32) + from_side[rows].astype(F32)

        @pl.when(kind == 0)
        def _():
            result[rows] = (tok_l + total).astype(BF16)

        @pl.when(kind == 1)
        def _():
            scaled, inverse = layer_norm(tok_l)
            grad = total * gain_ref[...]
            mean_grad = jnp.mean(grad, axis=-1, keepdims=True)
            mean_mixed = jnp.mean(grad * scaled, axis=-1, keepdims=True)
            result[rows] = (cot_l + (grad - mean_grad - scaled * mean_mixed) * inverse).astype(BF16)

    def share(chunk):
        rows = pl.ds(*chunks[chunk])
        return start([
            remote(final.at[kind, core, rows], final.at[kind, core, rows], side),
            remote(final.at[kind, core, rows], final.at[kind, core, rows], sibling),
        ])

    def relay(chunk, copy):
        rows = pl.ds(*chunks[chunk])
        copy.wait_recv()
        return start([remote(final.at[1 - kind, core, rows], final.at[1 - kind, core, rows], sibling)])[0]

    outs = []

    def place(k, lv):
        fields[k, lv] = dot(natural_ref[...], final[k, lv]).astype(BF16)
        for index, ref in enumerate((layer_ref, dtok_ref)):
            @pl.when(k == index)
            def _():
                pltpu.make_async_copy(fields.at[k, lv], ref.at[lv], out_sem.at[len(outs)]).start()
        outs.append(pltpu.make_async_copy(fields.at[k, lv], layer_ref.at[lv], out_sem.at[len(outs)]))

    finish(0)
    spread_out[...] = dot(spread_ref[...], result[0:T_AWAY]).astype(BF16)
    returned = start([
        remote(spread_out.at[pl.ds(at, size)], back.at[pl.ds(at, size)], target)
        for at, size, target in ((0, 64, {"lat": lat_up}), (64, 32, {"lon": lon_up}), (96, 32, {"lat": lat_up, "lon": lon_up}))
    ])
    finish(1)
    final[kind, core, T_AWAY:T_ROWS] = result[T_AWAY:T_ROWS]
    shared = [share(1)]
    second(1)
    for copy in returned:
        copy.wait_recv()
    final[kind, core, 0:T_AWAY] = dot(gather_ref[...], back[...]).astype(BF16)
    shared = [share(0)] + shared
    place(kind, core)
    second(0)
    relayed = [relay(1, shared[1][0])]
    second(2)
    third(1)
    relayed.append(relay(0, shared[0][0]))
    place(1 - kind, core)
    for _, copy in shared:
        copy.wait_recv()
    place(kind, 1 - core)
    third(0)
    for copy in relayed:
        copy.wait_recv()
    place(1 - kind, 1 - core)
    second(3)
    third(2)
    last(1)
    last(0)
    third(3)
    last(2)
    last(3)
    for copy in started:
        copy.wait_send()
    for copy in outs:
        copy.wait()


def finisher(layer_in, dtok_in, gqkv_in, gout_in, layer_out, dtok_out, gqkv_out, gout_out, turned, sem):
    copies = [
        pltpu.make_async_copy(src, dst, sem.at[i])
        for i, (src, dst) in enumerate(((layer_in, layer_out), (dtok_in, dtok_out), (gqkv_in, gqkv_out)))
    ]
    for copy in copies:
        copy.start()
    turned[0 : gout_in.shape[0], :] = gout_in[...]
    gout_out[...] = turned[...].T[:, 0 : gout_in.shape[0]]
    for copy in copies:
        copy.wait()


def body(tokens, norm_gain, w_qkv, w_out, bias_table, cotangent):
    nlon, nlat = lax.axis_size("lon"), lax.axis_size("lat")
    nz = nlon // 2
    width = tokens.shape[-1]
    rows = width // (nlon * nlat)
    half = CELLS // LEV
    vmem = pl.BlockSpec(memory_space=pltpu.VMEM)
    hbm = pl.BlockSpec(memory_space=pl.ANY)
    copies = 4 + 4 + 4 * (nlat - 1 + nz - 1 + 1) + 2 + 2 + 3 + 6
    shape = lambda *dims: pltpu.VMEM(dims, BF16)
    outs = (
        jax.ShapeDtypeStruct((LEV, half, width), BF16),
        jax.ShapeDtypeStruct((LEV, half, width), BF16),
        jax.ShapeDtypeStruct((rows, 768), F32),
    )
    results = pl.pallas_call(
        functools.partial(kernel, nlon, nlat),
        out_shape=outs + (jax.ShapeDtypeStruct((rows, 256), F32),),
        in_specs=[vmem] * 15,
        out_specs=(hbm, hbm, vmem, vmem),
        scratch_shapes=[
            shape(2, G_ROWS - 112, width),
            shape(2, G_ROWS, width),
            shape(CELLS, width),
            shape(CELLS, width),
            shape(CELLS, width),
            shape(width, CELLS),
            shape(width, CELLS),
            shape(CELLS, 768),
            shape(CELLS, 256),
            pltpu.VMEM((768, 128), F32),
            pltpu.VMEM((WINDOW, SEL), F32),
            pltpu.VMEM((4, WINDOW, WINDOW), F32),
            shape(CELLS, 768),
            shape(CELLS, 256),
            shape(4, 2, nz, nlat, rows, 256),
            shape(3, nlat - 1, 2, nz, rows, 256),
            shape(3, 2, nz, rows, 256),
            shape(max(nz - 1, 1), 2, nlat, rows, 256),
            shape(2, nlat, rows, 256),
            shape(3, max(nz - 1, 1), 2, rows, 256),
            shape(nlat - 1, 2, rows, 256),
            shape(4, 2, rows, 256),
            shape(4, rows, 256),
            shape(LEV, 2, T_ROWS, width),
            shape(2, T_ROWS, width),
            shape(T_ROWS, width),
            shape(T_ROWS, width),
            shape(T_ROWS, width),
            shape(U_ROWS, width),
            shape(U_ROWS, width),
            shape(2, LEV, T_ROWS, width),
            shape(2, LEV, half, width),
            pltpu.SemaphoreType.DMA((copies,)),
            pltpu.SemaphoreType.DMA((copies,)),
            pltpu.SemaphoreType.DMA((4,)),
        ],
        compiler_params=pltpu.CompilerParams(
            collective_id=0, has_side_effects=True, vmem_limit_bytes=56 * 1024 * 1024
        ),
    )(
        tokens.reshape(CELLS, width), cotangent.reshape(CELLS, width), norm_gain.reshape(1, width),
        w_qkv, w_out, bias_table, *[jnp.asarray(t) for t in tables()],
    )
    layer, dtok, gqkv, gout = pl.pallas_call(
        finisher,
        out_shape=outs + (jax.ShapeDtypeStruct((256, rows), F32),),
        in_specs=[hbm, hbm, hbm, vmem],
        out_specs=(hbm, hbm, hbm, vmem),
        scratch_shapes=[pltpu.VMEM((max(128, rows), 256), F32), pltpu.SemaphoreType.DMA((3,))],
    )(*results)
    field = (LEV, WLAT, LON, width)
    return layer.reshape(field), dtok.reshape(field), gqkv, gout


def solution(mesh):
    in_specs = (
        P(None, "lat", "lon", None),
        P(),
        P(None, "head"),
        P("head", None),
        P(None, "head"),
        P(None, "lat", "lon", None),
    )
    out_specs = (
        P(None, "lat", "lon", None),
        P(None, "lat", "lon", None),
        P(("lon", "lat"), "head"),
        P("head", ("lon", "lat")),
    )
    return jax.shard_map(body, mesh=mesh, in_specs=in_specs, out_specs=out_specs, check_vma=False)
```

```python
import functools

import jax
import jax.numpy as jnp
import ml_dtypes
import numpy as np
from jax import lax
from jax.experimental import pallas as pl
from jax.experimental.pallas import tpu as pltpu
from jax.sharding import PartitionSpec as P

MESH = pl.DeviceIdType.MESH
HEAD_DIM = 64
LEV = 2
WLAT = 6
WLON = 12
LON = 24
WINDOW = LEV * WLAT * WLON
CELLS = LEV * WLAT * LON
EPSILON = 1e-05
NEG_FILL = -1e30
F32 = jnp.float32
BF16 = jnp.bfloat16

G_START = (0, 112, 224, 272)
G_ROWS = 320
T_START = (90, 0, 54, 72)
T_AWAY = 96
T_ROWS = 144
U_START = (None, 0, 64, 96)
U_ROWS = 128
SEL = 384


def quarter(row, col):
    down, right = row >= 3, col >= 18
    part = (2 if right else 0) + (1 if down else 0)
    width = 6 if right else 18
    return part, (row % 3) * width + (col - 18 if right else col), 3 * width


def tables():
    own = np.zeros((G_ROWS, CELLS), np.float32)
    compact = np.zeros((CELLS, G_ROWS), np.float32)
    level = np.zeros((LEV, T_ROWS, CELLS), np.float32)
    spread = np.zeros((U_ROWS, T_AWAY), np.float32)
    gather = np.zeros((T_AWAY, U_ROWS + T_AWAY), np.float32)
    natural = np.zeros((CELLS // LEV, T_ROWS), np.float32)
    for lv in range(LEV):
        for row in range(WLAT):
            for col in range(LON):
                part, index, size = quarter(row, col)
                held = G_START[part] + lv * size + index
                src_row = row + 3 if row < 3 else row - 3
                src_col = col + 6 if col < 18 else col - 18
                own[held, lv * 144 + src_row * LON + src_col] = 1
                place = (col // WLON) * WINDOW + lv * 72 + row * WLON + col % WLON
                compact[place, held] = 1
                level[lv, T_START[part] + index, place] = 1
                if lv == 0:
                    natural[src_row * LON + src_col, T_START[part] + index] = 1
                    if part:
                        spread[U_START[part] + index, T_START[part] + index] = 1
                        gather[T_START[part] + index, U_START[part] + index] = 1
                    elif index < 6:
                        gather[T_START[part] + index, U_ROWS + T_START[part] + index] = 1
    select = np.zeros((SEL, WINDOW), np.float32)
    for i in range(WINDOW):
        select[(i // 72) * 253 + (i // WLON % WLAT) * 23 + i % WLON, i] = 1
    half = np.arange(WINDOW) // WLON % WLAT >= 3
    cross = (half[:, None] != half[None, :]).astype(np.float32)
    exact = [t.astype(ml_dtypes.bfloat16) for t in (own, compact, level, spread, gather, natural, select, np.eye(128, dtype=np.float32))]
    return exact + [cross]


def dot(a, b, ca=1, cb=0):
    return lax.dot_general(a, b, (((ca,), (cb,)), ((), ())), preferred_element_type=F32)


def layer_norm(floats):
    center = floats - jnp.mean(floats, axis=-1, keepdims=True)
    inverse = lax.rsqrt(jnp.mean(center * center, axis=-1, keepdims=True) + EPSILON)
    return center * inverse, inverse


def kernel(
    nlon, nlat,
    tok_in, cot_in, own_in, table_in, select_in, cross_in, compact_in, gain_in, wqkv_in, wout_in, eye_in,
    level_in, spread_in, gather_in, natural_in,
    field_ref, gqkv_ref, gout_ref,
    sent, held, tokc, cotc, normed, normed_t, cot_t, qkv, datt, wide_table, rolled, bias, dqkv, att,
    wgt, near_x, sum_x, near_z, first_z, sum_z, last_x, sum_y, from_y,
    term, from_core, to_side, from_side, result, spread_out, back, final,
    tok_ref, cot_ref, own_ref, table_ref, select_ref, cross_ref, compact_ref, gain_ref, wqkv_ref, wout_ref, eye_ref,
    level_ref, spread_ref, gather_ref, natural_ref,
    send_sem, recv_sem, in_sem,
):
    lon, lat, head = lax.axis_index("lon"), lax.axis_index("lat"), lax.axis_index("head")
    nz = nlon // 2
    y_hi, z = lon // nz, lon % nz
    kind, core = head // 2, head % 2
    lat_up, lat_down = (lat + 1) % nlat, (lat + nlat - 1) % nlat
    lon_up, lon_down = (lon + 1) % nlon, (lon + nlon - 1) % nlon
    sibling = {"head": kind * 2 + 1 - core}
    side = {"head": (1 - kind) * 2 + core}
    x_up = [{"lat": (lat + d) % nlat} for d in range(1, nlat)]
    x_down = [{"lat": (lat + nlat - d) % nlat} for d in range(1, nlat)]
    z_up = [{"lon": y_hi * nz + (z + d) % nz} for d in range(1, nz)]
    z_down = [{"lon": y_hi * nz + (z + nz - d) % nz} for d in range(1, nz)]
    far = {"lon": (1 - y_hi) * nz + z}

    sources = x_down + z_down + [
        far, sibling, side,
        {"lon": lon_up}, {"lon": lon_down},
        {"lat": lat_up, "lon": lon_up}, {"lat": lat_down, "lon": lon_down},
    ]
    barrier = pltpu.get_barrier_semaphore()
    for source in sources:
        pl.semaphore_signal(barrier, inc=1, device_id=source, device_id_type=MESH)

    loads = [
        pltpu.make_async_copy(src, dst, in_sem.at[i])
        for i, (src, dst) in enumerate((
            (tok_in, tok_ref), (cot_in, cot_ref), (own_in, own_ref), (table_in, table_ref), (select_in, select_ref),
            (cross_in, cross_ref), (compact_in, compact_ref), (gain_in, gain_ref), (wqkv_in, wqkv_ref), (wout_in, wout_ref),
            (eye_in, eye_ref), (level_in, level_ref), (spread_in, spread_ref), (gather_in, gather_ref), (natural_in, natural_ref),
        ))
    ]
    for load in loads:
        load.start()
    for load in loads[:3]:
        load.wait()

    count = [0]

    def remote(src, dst, target):
        index = count[0]
        count[0] += 1
        return pltpu.make_async_remote_copy(
            src_ref=src, dst_ref=dst, send_sem=send_sem.at[index], recv_sem=recv_sem.at[index],
            device_id=target, device_id_type=MESH,
        )

    started = []

    def start(copies):
        for copy in copies:
            copy.start()
        started.extend(copies)
        return copies

    for i, ref in enumerate((tok_ref, cot_ref)):
        arranged = dot(own_ref[...], ref[...]).astype(BF16)
        held[i, 0:112] = arranged[0:112]
        sent[i] = arranged[112:]
    pl.semaphore_wait(barrier, len(sources))
    diagonal = {"lat": lat_down, "lon": lon_down}
    parts = [(112, 64, {"lat": lat_down}), (224, 48, {"lon": lon_down}), (272, 48, diagonal), (176, 48, {"lat": lat_down})]
    shifted = start([
        remote(sent.at[core, pl.ds(at - 112, size)], held.at[core, pl.ds(at, size)], target) for at, size, target in parts
    ])

    for load in loads[3:]:
        load.wait()

    wide_table[...] = jnp.zeros(wide_table.shape, F32)
    wide_table[0:4, 0 : table_ref.shape[1]] = table_ref[...]
    turned = wide_table[...]
    for h in range(4):
        stepped = jnp.broadcast_to(turned[h : h + 1, :], (16, turned.shape[1]))
        stepped = pltpu.roll(stepped, 0, 1, stride=1, stride_axis=0)
        for step in range(LEV * WLAT):
            offset = (step // WLAT) * 253 + (step % WLAT) * 23
            shift = (offset - 379) % turned.shape[1]
            moved = pltpu.roll(stepped, shift, 1)
            rolled[WLON * step : WLON * step + WLON, :] = moved[0:WLON, 0:SEL]
        rest = rolled[...]
        total = jnp.zeros((WINDOW, WINDOW), F32)
        for _ in range(3):
            piece = rest.astype(BF16)
            rest = rest - piece.astype(F32)
            total = total + dot(piece, select_ref[...])
        excluded = (cross_ref[...] > 0.5) & (lat == nlat - 1)
        bias[h] = jnp.where(excluded, NEG_FILL, total)

    forwards = []
    for copy, (at, size, _) in zip(shifted, parts):
        copy.wait_recv()
        forwards += start([remote(held.at[core, pl.ds(at, size)], held.at[core, pl.ds(at, size)], sibling)])
    for copy in forwards:
        copy.wait_recv()

    tokc[...] = dot(compact_ref[...], held[0]).astype(BF16)
    cotc[...] = dot(compact_ref[...], held[1]).astype(BF16)
    for at in range(0, CELLS, 48):
        scaled, _ = layer_norm(tokc[at : at + 48, :].astype(F32))
        normed[at : at + 48, :] = (scaled * gain_ref[...]).astype(BF16)
    qkv[...] = dot(normed[...], wqkv_ref[...]).astype(BF16)
    datt[...] = dot(cotc[...], wout_ref[...], 1, 1).astype(BF16)
    for at in range(0, normed.shape[1], 128):
        normed_t[at : at + 128, :] = dot(eye_ref[...], normed[:, at : at + 128], 1, 1).astype(BF16)
        cot_t[at : at + 128, :] = dot(eye_ref[...], cotc[:, at : at + 128], 1, 1).astype(BF16)

    def attend(w, h):
        rows = pl.ds(w * WINDOW, WINDOW)
        first = 3 * HEAD_DIM * h
        query = qkv[rows, first : first + 64]
        key = qkv[rows, first + 64 : first + 128]
        value = qkv[rows, first + 128 : first + 192]
        grad = datt[rows, 64 * h : 64 * h + 64]
        scores = dot(key, query, 1, 1) * (HEAD_DIM ** -0.5) + bias[h]
        raised = jnp.exp(scores - jnp.max(scores, axis=0, keepdims=True))
        prob = raised * (1.0 / jnp.sum(raised, axis=0, keepdims=True))
        half = prob.astype(BF16)
        grad_prob = dot(value, grad, 1, 1)
        row_term = jnp.sum(prob * grad_prob, axis=0, keepdims=True)
        grad_score = (prob * (grad_prob - row_term) * (HEAD_DIM ** -0.5)).astype(BF16)
        att[rows, 64 * h : 64 * h + 64] = dot(half, value, 0, 0).astype(BF16)
        dqkv[rows, first : first + 64] = dot(grad_score, key, 0, 0).astype(BF16)
        dqkv[rows, first + 64 : first + 128] = dot(grad_score, query, 1, 0).astype(BF16)
        dqkv[rows, first + 128 : first + 192] = dot(half, grad, 1, 0).astype(BF16)

    rows_out = wgt.shape[4]
    on_first, on_second, on_y = {}, {}, {}

    def weight(h):
        wide = dot(normed_t[...], dqkv[:, 192 * h : 192 * h + 192]).astype(BF16)
        wgt[h, :, :, :, :, 0:192] = wide.reshape(2, nz, nlat, rows_out, 192)
        narrow = dot(cot_t[...], att[:, 64 * h : 64 * h + 64]).astype(BF16)
        wgt[h, :, :, :, :, 192:256] = narrow.reshape(2, nz, nlat, rows_out, 64)

    def leave(h):
        if h == 0:
            on_first[h] = start([
                remote(wgt.at[h, :, target["lon"] - y_hi * nz], near_z.at[d], target) for d, target in enumerate(z_up)
            ])
        else:
            on_first[h] = start([
                remote(wgt.at[h, :, :, target["lat"]], near_x.at[h - 1, d], target) for d, target in enumerate(x_up)
            ])

    def second(h):
        for copy in on_first[h]:
            copy.wait_recv()
        if h == 0:
            total = wgt[h, :, z].astype(F32)
            for d in range(nz - 1):
                total = total + near_z[d].astype(F32)
            first_z[...] = total.astype(BF16)
            on_second[h] = start([
                remote(first_z.at[:, target["lat"]], last_x.at[d], target) for d, target in enumerate(x_up)
            ])
        else:
            total = wgt[h, :, :, lat].astype(F32)
            for d in range(nlat - 1):
                total = total + near_x[h - 1, d].astype(F32)
            sum_x[h - 1] = total.astype(BF16)
            on_second[h] = start([
                remote(sum_x.at[h - 1, :, target["lon"] - y_hi * nz], sum_z.at[h - 1, d], target) for d, target in enumerate(z_up)
            ])

    def third(h):
        for copy in on_second[h]:
            copy.wait_recv()
        if h == 0:
            total = first_z[:, lat].astype(F32)
            for d in range(nlat - 1):
                total = total + last_x[d].astype(F32)
        else:
            total = sum_x[h - 1, :, z].astype(F32)
            for d in range(nz - 1):
                total = total + sum_z[h - 1, d].astype(F32)
        sum_y[h] = total.astype(BF16)
        on_y[h] = start([remote(sum_y.at[h, 1 - y_hi], from_y.at[h], far)])[0]

    def last(h):
        on_y[h].wait_recv()
        total = sum_y[h, y_hi].astype(F32) + from_y[h].astype(F32)
        gqkv_ref[:, 192 * h : 192 * h + 192] = total[:, 0:192]
        gout_ref[:, 64 * h : 64 * h + 64] = total[:, 192:256]

    for h in range(4):
        for w in range(2):
            attend(w, h)
        if h < 3:
            weight(h)
            leave(h)

    chunks = ((0, T_AWAY), (T_AWAY, T_ROWS - T_AWAY))
    on_core = []
    for lv in (1 - core, core):
        for at, size in chunks:
            order = level_ref[lv, at : at + size]
            att_l = dot(order, att[...]).astype(BF16)
            dqkv_l = dot(order, dqkv[...]).astype(BF16)
            term[lv, 0, at : at + size] = dot(att_l, wout_ref[...]).astype(BF16)
            term[lv, 1, at : at + size] = dot(dqkv_l, wqkv_ref[...], 1, 1).astype(BF16)
            if lv is not core:
                on_core += start([
                    remote(term.at[1 - core, :, pl.ds(at, size)], from_core.at[:, pl.ds(at, size)], sibling)
                ])
    on_side = []
    for copy, (at, size) in zip(on_core, chunks):
        copy.wait_recv()
        rows = pl.ds(at, size)
        to_side[rows] = (term[core, 1 - kind, rows].astype(F32) + from_core[1 - kind, rows].astype(F32)).astype(BF16)
        on_side += start([remote(to_side.at[rows], from_side.at[rows], side)])
    weight(3)

    def finish(chunk):
        at, size = chunks[chunk]
        rows = pl.ds(at, size)
        tok_l = dot(level_ref[core, at : at + size], tokc[...])
        cot_l = dot(level_ref[core, at : at + size], cotc[...])
        on_side[chunk].wait_recv()
        total = term[core, kind, rows].astype(F32) + from_core[kind, rows].astype(F32) + from_side[rows].astype(F32)

        @pl.when(kind == 0)
        def _():
            result[rows] = (tok_l + total).astype(BF16)

        @pl.when(kind == 1)
        def _():
            scaled, inverse = layer_norm(tok_l)
            grad = total * gain_ref[...]
            mean_grad = jnp.mean(grad, axis=-1, keepdims=True)
            mean_mixed = jnp.mean(grad * scaled, axis=-1, keepdims=True)
            result[rows] = (cot_l + (grad - mean_grad - scaled * mean_mixed) * inverse).astype(BF16)

    def share(chunk):
        rows = pl.ds(*chunks[chunk])
        return start([
            remote(final.at[kind, core, rows], final.at[kind, core, rows], side),
            remote(final.at[kind, core, rows], final.at[kind, core, rows], sibling),
        ])

    def relay(chunk, copy):
        rows = pl.ds(*chunks[chunk])
        copy.wait_recv()
        return start([remote(final.at[1 - kind, core, rows], final.at[1 - kind, core, rows], sibling)])[0]

    def place(k, lv):
        field_ref[k, lv] = dot(natural_ref[...], final[k, lv]).astype(BF16)

    second(1)
    finish(0)
    spread_out[...] = dot(spread_ref[...], result[0:T_AWAY]).astype(BF16)
    returned = start([
        remote(spread_out.at[pl.ds(at, size)], back.at[pl.ds(at, size)], target)
        for at, size, target in ((0, 64, {"lat": lat_up}), (64, 32, {"lon": lon_up}), (96, 32, {"lat": lat_up, "lon": lon_up}))
    ])
    leave(3)
    finish(1)
    final[kind, core, T_AWAY:T_ROWS] = result[T_AWAY:T_ROWS]
    shared = [share(1)]
    second(0)
    second(2)
    third(1)
    relayed = [relay(1, shared[0][0])]
    for copy in returned:
        copy.wait_recv()
    back[U_ROWS : U_ROWS + T_AWAY] = result[0:T_AWAY]
    final[kind, core, 0:T_AWAY] = dot(gather_ref[...], back[...]).astype(BF16)
    shared = [share(0)] + shared
    place(kind, core)
    third(2)
    third(0)
    second(3)
    relayed.append(relay(0, shared[0][0]))
    place(1 - kind, core)
    last(1)
    for _, copy in shared:
        copy.wait_recv()
    place(kind, 1 - core)
    third(3)
    for copy in relayed:
        copy.wait_recv()
    place(1 - kind, 1 - core)
    last(0)
    last(2)
    last(3)
    for copy in started:
        copy.wait_send()


def finisher(fields, gqkv_in, gout_in, layer_out, dtok_out, gqkv_out, gout_out, sem):
    copies = [
        pltpu.make_async_copy(src, dst, sem.at[i])
        for i, (src, dst) in enumerate((
            (fields.at[0], layer_out), (fields.at[1], dtok_out), (gqkv_in, gqkv_out), (gout_in, gout_out),
        ))
    ]
    for copy in copies:
        copy.start()
    for copy in copies:
        copy.wait()


def body(tokens, norm_gain, w_qkv, w_out, bias_table, cotangent):
    nlon, nlat = lax.axis_size("lon"), lax.axis_size("lat")
    nz = nlon // 2
    width = tokens.shape[-1]
    rows = width // (nlon * nlat)
    half = CELLS // LEV
    vmem = pl.BlockSpec(memory_space=pltpu.VMEM)
    hbm = pl.BlockSpec(memory_space=pl.ANY)
    copies = 4 + 4 + 4 * (nlat - 1 + nz - 1 + 1) + 2 + 2 + 3 + 6
    shape = lambda *dims: pltpu.VMEM(dims, BF16)
    outs = (
        jax.ShapeDtypeStruct((LEV, half, width), BF16),
        jax.ShapeDtypeStruct((LEV, half, width), BF16),
        jax.ShapeDtypeStruct((rows, 768), F32),
        jax.ShapeDtypeStruct((rows, 256), F32),
    )
    own, compact, level, spread, gather, natural, select, eye, cross = [jnp.asarray(t) for t in tables()]
    operands = (
        tokens.reshape(CELLS, width), cotangent.reshape(CELLS, width), own, bias_table.T, select, cross, compact,
        norm_gain.reshape(1, width), w_qkv, w_out, eye, level, spread, gather, natural,
    )
    results = pl.pallas_call(
        functools.partial(kernel, nlon, nlat),
        out_shape=(pltpu.VMEM((2, LEV, half, width), BF16), pltpu.VMEM((rows, 768), F32), pltpu.VMEM((rows, 256), F32)),
        in_specs=[hbm] * 15,
        out_specs=(vmem, vmem, vmem),
        scratch_shapes=[
            shape(2, G_ROWS - 112, width),
            shape(2, G_ROWS, width),
            shape(CELLS, width),
            shape(CELLS, width),
            shape(CELLS, width),
            shape(width, CELLS),
            shape(width, CELLS),
            shape(CELLS, 768),
            shape(CELLS, 256),
            pltpu.VMEM((8, 768), F32),
            pltpu.VMEM((WINDOW, SEL), F32),
            pltpu.VMEM((4, WINDOW, WINDOW), F32),
            shape(CELLS, 768),
            shape(CELLS, 256),
            shape(4, 2, nz, nlat, rows, 256),
            shape(3, nlat - 1, 2, nz, rows, 256),
            shape(3, 2, nz, rows, 256),
            shape(max(nz - 1, 1), 2, nlat, rows, 256),
            shape(2, nlat, rows, 256),
            shape(3, max(nz - 1, 1), 2, rows, 256),
            shape(nlat - 1, 2, rows, 256),
            shape(4, 2, rows, 256),
            shape(4, rows, 256),
            shape(LEV, 2, T_ROWS, width),
            shape(2, T_ROWS, width),
            shape(T_ROWS, width),
            shape(T_ROWS, width),
            shape(T_ROWS, width),
            shape(U_ROWS, width),
            shape(U_ROWS + T_AWAY, width),
            shape(2, LEV, T_ROWS, width),
            *[pltpu.VMEM(x.shape, x.dtype) for x in operands],
            pltpu.SemaphoreType.DMA((copies,)),
            pltpu.SemaphoreType.DMA((copies,)),
            pltpu.SemaphoreType.DMA((len(operands),)),
        ],
        compiler_params=pltpu.CompilerParams(
            collective_id=0, has_side_effects=True, vmem_limit_bytes=56 * 1024 * 1024
        ),
    )(*operands)
    layer, dtok, gqkv, gout = pl.pallas_call(
        finisher,
        out_shape=outs,
        in_specs=[vmem] * 3,
        out_specs=(hbm,) * 4,
        scratch_shapes=[pltpu.SemaphoreType.DMA((4,))],
    )(*results)
    field = (LEV, WLAT, LON, width)
    return layer.reshape(field), dtok.reshape(field), gqkv, gout.T


def solution(mesh):
    in_specs = (
        P(None, "lat", "lon", None),
        P(),
        P(None, "head"),
        P("head", None),
        P(None, "head"),
        P(None, "lat", "lon", None),
    )
    out_specs = (
        P(None, "lat", "lon", None),
        P(None, "lat", "lon", None),
        P(("lon", "lat"), "head"),
        P("head", ("lon", "lat")),
    )
    return jax.shard_map(body, mesh=mesh, in_specs=in_specs, out_specs=out_specs, check_vma=False)
```

```python
import functools

import jax
import jax.numpy as jnp
import ml_dtypes
import numpy as np
from jax import lax
from jax.experimental import pallas as pl
from jax.experimental.pallas import tpu as pltpu
from jax.sharding import PartitionSpec as P

MESH = pl.DeviceIdType.MESH
HEAD_DIM = 64
LEV = 2
WLAT = 6
WLON = 12
LON = 24
WINDOW = LEV * WLAT * WLON
CELLS = LEV * WLAT * LON
EPSILON = 1e-05
NEG_FILL = -1e30
F32 = jnp.float32
BF16 = jnp.bfloat16

G_START = (0, 112, 224, 272)
G_ROWS = 320
T_START = (90, 0, 54, 72)
T_ROWS = 144
CHUNK = 48
U_START = (None, 0, 16, 48)
U_ROWS = 80
SEL = 384


def quarter(row, col):
    down, right = row >= 3, col >= 18
    part = (2 if right else 0) + (1 if down else 0)
    width = 6 if right else 18
    return part, (row % 3) * width + (col - 18 if right else col), 3 * width


def tables():
    own = np.zeros((G_ROWS, CELLS), np.float32)
    compact = np.zeros((CELLS, G_ROWS), np.float32)
    level = np.zeros((LEV, T_ROWS, CELLS), np.float32)
    spread = np.zeros((U_ROWS, CHUNK), np.float32)
    gather = np.zeros((CHUNK, U_ROWS + CHUNK), np.float32)
    natural = np.zeros((CELLS // LEV, T_ROWS), np.float32)
    for lv in range(LEV):
        for row in range(WLAT):
            for col in range(LON):
                part, index, size = quarter(row, col)
                held = G_START[part] + lv * size + index
                src_row = row + 3 if row < 3 else row - 3
                src_col = col + 6 if col < 18 else col - 18
                own[held, lv * 144 + src_row * LON + src_col] = 1
                place = (col // WLON) * WINDOW + lv * 72 + row * WLON + col % WLON
                compact[place, held] = 1
                level[lv, T_START[part] + index, place] = 1
                if lv == 0:
                    natural[src_row * LON + src_col, T_START[part] + index] = 1
                    at = T_START[part] + index - CHUNK
                    if 0 <= at < CHUNK and part:
                        travel = U_START[part] + (at if part == 1 else index)
                        spread[travel, at] = 1
                        gather[at, travel] = 1
                    elif 0 <= at < CHUNK:
                        gather[at, U_ROWS + at] = 1
    select = np.zeros((SEL, WINDOW), np.float32)
    for i in range(WINDOW):
        select[(i // 72) * 253 + (i // WLON % WLAT) * 23 + i % WLON, i] = 1
    half = np.arange(WINDOW) // WLON % WLAT >= 3
    cross = (half[:, None] != half[None, :]).astype(np.float32)
    exact = [t.astype(ml_dtypes.bfloat16) for t in (own, compact, level, spread, gather, natural, select, np.eye(128, dtype=np.float32))]
    return exact + [cross]


def dot(a, b, ca=1, cb=0):
    return lax.dot_general(a, b, (((ca,), (cb,)), ((), ())), preferred_element_type=F32)


def layer_norm(floats):
    center = floats - jnp.mean(floats, axis=-1, keepdims=True)
    inverse = lax.rsqrt(jnp.mean(center * center, axis=-1, keepdims=True) + EPSILON)
    return center * inverse, inverse


def kernel(
    nlon, nlat,
    tok_in, cot_in, own_in, table_in, select_in, cross_in, compact_in, gain_in, wqkv_in, wout_in, eye_in,
    level_in, spread_in, gather_in, natural_in,
    layer_ref, dtok_ref, gqkv_ref, gout_ref,
    sent, held, tokc, cotc, normed, normed_t, cot_t, qkv, datt, wide_table, rolled, bias, dqkv, att,
    wgt, near_x, sum_x, near_z, first_z, sum_z, last_x, sum_y, from_y,
    term, from_core, to_side, from_side, tok_l, cot_l, result, spread_out, back, final,
    tok_ref, cot_ref, own_ref, table_ref, select_ref, cross_ref, compact_ref, gain_ref, wqkv_ref, wout_ref, eye_ref,
    level_ref, spread_ref, gather_ref, natural_ref,
    send_sem, recv_sem, in_sem,
):
    lon, lat, head = lax.axis_index("lon"), lax.axis_index("lat"), lax.axis_index("head")
    nz = nlon // 2
    y_hi, z = lon // nz, lon % nz
    kind, core = head // 2, head % 2
    lat_up, lat_down = (lat + 1) % nlat, (lat + nlat - 1) % nlat
    lon_up, lon_down = (lon + 1) % nlon, (lon + nlon - 1) % nlon
    sibling = {"head": kind * 2 + 1 - core}
    side = {"head": (1 - kind) * 2 + core}
    x_up = [{"lat": (lat + d) % nlat} for d in range(1, nlat)]
    x_down = [{"lat": (lat + nlat - d) % nlat} for d in range(1, nlat)]
    z_up = [{"lon": y_hi * nz + (z + d) % nz} for d in range(1, nz)]
    z_down = [{"lon": y_hi * nz + (z + nz - d) % nz} for d in range(1, nz)]
    far = {"lon": (1 - y_hi) * nz + z}

    sources = x_down + z_down + [
        far, sibling, side,
        {"lon": lon_up}, {"lon": lon_down},
        {"lat": lat_up, "lon": lon_up}, {"lat": lat_down, "lon": lon_down},
    ]
    barrier = pltpu.get_barrier_semaphore()
    for source in sources:
        pl.semaphore_signal(barrier, inc=1, device_id=source, device_id_type=MESH)

    loads = [
        pltpu.make_async_copy(src, dst, in_sem.at[i])
        for i, (src, dst) in enumerate((
            (tok_in, tok_ref), (cot_in, cot_ref), (own_in, own_ref), (table_in, table_ref), (select_in, select_ref),
            (cross_in, cross_ref), (compact_in, compact_ref), (gain_in, gain_ref), (wqkv_in, wqkv_ref), (wout_in, wout_ref),
            (eye_in, eye_ref), (level_in, level_ref), (spread_in, spread_ref), (gather_in, gather_ref), (natural_in, natural_ref),
        ))
    ]
    for load in loads:
        load.start()
    for load in loads[:3]:
        load.wait()

    count = [0]

    def remote(src, dst, target):
        index = count[0]
        count[0] += 1
        return pltpu.make_async_remote_copy(
            src_ref=src, dst_ref=dst, send_sem=send_sem.at[index], recv_sem=recv_sem.at[index],
            device_id=target, device_id_type=MESH,
        )

    started = []

    def start(copies):
        for copy in copies:
            copy.start()
        started.extend(copies)
        return copies

    for i, ref in enumerate((tok_ref, cot_ref)):
        arranged = dot(own_ref[...], ref[...]).astype(BF16)
        held[i, 0:112] = arranged[0:112]
        sent[i] = arranged[112:]
    pl.semaphore_wait(barrier, len(sources))
    diagonal = {"lat": lat_down, "lon": lon_down}
    parts = [(112, 64, {"lat": lat_down}), (224, 48, {"lon": lon_down}), (272, 48, diagonal), (176, 48, {"lat": lat_down})]
    shifted = start([
        remote(sent.at[core, pl.ds(at - 112, size)], held.at[core, pl.ds(at, size)], target) for at, size, target in parts
    ])

    for load in loads[3:]:
        load.wait()

    wide_table[...] = jnp.zeros(wide_table.shape, F32)
    wide_table[0:4, 0 : table_ref.shape[1]] = table_ref[...]
    turned = wide_table[...]
    for h in range(4):
        stepped = jnp.broadcast_to(turned[h : h + 1, :], (16, turned.shape[1]))
        stepped = pltpu.roll(stepped, 0, 1, stride=1, stride_axis=0)
        for step in range(LEV * WLAT):
            offset = (step // WLAT) * 253 + (step % WLAT) * 23
            shift = (offset - 379) % turned.shape[1]
            moved = pltpu.roll(stepped, shift, 1)
            rolled[WLON * step : WLON * step + WLON, :] = moved[0:WLON, 0:SEL]
        rest = rolled[...]
        total = jnp.zeros((WINDOW, WINDOW), F32)
        for _ in range(3):
            piece = rest.astype(BF16)
            rest = rest - piece.astype(F32)
            total = total + dot(piece, select_ref[...])
        excluded = (cross_ref[...] > 0.5) & (lat == nlat - 1)
        bias[h] = jnp.where(excluded, NEG_FILL, total)

    forwards = []
    for copy, (at, size, _) in zip(shifted, parts):
        copy.wait_recv()
        forwards += start([remote(held.at[core, pl.ds(at, size)], held.at[core, pl.ds(at, size)], sibling)])
    for copy in forwards:
        copy.wait_recv()

    tokc[...] = dot(compact_ref[...], held[0]).astype(BF16)
    cotc[...] = dot(compact_ref[...], held[1]).astype(BF16)
    for at in range(0, CELLS, 48):
        scaled, _ = layer_norm(tokc[at : at + 48, :].astype(F32))
        normed[at : at + 48, :] = (scaled * gain_ref[...]).astype(BF16)
    qkv[...] = dot(normed[...], wqkv_ref[...]).astype(BF16)
    datt[...] = dot(cotc[...], wout_ref[...], 1, 1).astype(BF16)
    for at in range(0, normed.shape[1], 128):
        normed_t[at : at + 128, :] = dot(eye_ref[...], normed[:, at : at + 128], 1, 1).astype(BF16)
        cot_t[at : at + 128, :] = dot(eye_ref[...], cotc[:, at : at + 128], 1, 1).astype(BF16)

    def attend(w, h):
        rows = pl.ds(w * WINDOW, WINDOW)
        first = 3 * HEAD_DIM * h
        query = qkv[rows, first : first + 64]
        key = qkv[rows, first + 64 : first + 128]
        value = qkv[rows, first + 128 : first + 192]
        grad = datt[rows, 64 * h : 64 * h + 64]
        scores = dot(key, query, 1, 1) * (HEAD_DIM ** -0.5) + bias[h]
        raised = jnp.exp(scores - jnp.max(scores, axis=0, keepdims=True))
        prob = raised * (1.0 / jnp.sum(raised, axis=0, keepdims=True))
        half = prob.astype(BF16)
        grad_prob = dot(value, grad, 1, 1)
        row_term = jnp.sum(prob * grad_prob, axis=0, keepdims=True)
        grad_score = (prob * (grad_prob - row_term) * (HEAD_DIM ** -0.5)).astype(BF16)
        att[rows, 64 * h : 64 * h + 64] = dot(half, value, 0, 0).astype(BF16)
        dqkv[rows, first : first + 64] = dot(grad_score, key, 0, 0).astype(BF16)
        dqkv[rows, first + 64 : first + 128] = dot(grad_score, query, 1, 0).astype(BF16)
        dqkv[rows, first + 128 : first + 192] = dot(half, grad, 1, 0).astype(BF16)

    rows_out = wgt.shape[4]
    on_first, on_second, on_y = {}, {}, {}

    def weight(h):
        wide = dot(normed_t[...], dqkv[:, 192 * h : 192 * h + 192]).astype(BF16)
        wgt[h, :, :, :, :, 0:192] = wide.reshape(2, nz, nlat, rows_out, 192)
        narrow = dot(cot_t[...], att[:, 64 * h : 64 * h + 64]).astype(BF16)
        wgt[h, :, :, :, :, 192:256] = narrow.reshape(2, nz, nlat, rows_out, 64)

    def leave(h):
        if h == 0:
            on_first[h] = start([
                remote(wgt.at[h, :, target["lon"] - y_hi * nz], near_z.at[d], target) for d, target in enumerate(z_up)
            ])
        else:
            on_first[h] = start([
                remote(wgt.at[h, :, :, target["lat"]], near_x.at[h - 1, d], target) for d, target in enumerate(x_up)
            ])

    def second(h):
        for copy in on_first[h]:
            copy.wait_recv()
        if h == 0:
            total = wgt[h, :, z].astype(F32)
            for d in range(nz - 1):
                total = total + near_z[d].astype(F32)
            first_z[...] = total.astype(BF16)
            on_second[h] = start([
                remote(first_z.at[:, target["lat"]], last_x.at[d], target) for d, target in enumerate(x_up)
            ])
        else:
            total = wgt[h, :, :, lat].astype(F32)
            for d in range(nlat - 1):
                total = total + near_x[h - 1, d].astype(F32)
            sum_x[h - 1] = total.astype(BF16)
            on_second[h] = start([
                remote(sum_x.at[h - 1, :, target["lon"] - y_hi * nz], sum_z.at[h - 1, d], target) for d, target in enumerate(z_up)
            ])

    def third(h):
        for copy in on_second[h]:
            copy.wait_recv()
        if h == 0:
            total = first_z[:, lat].astype(F32)
            for d in range(nlat - 1):
                total = total + last_x[d].astype(F32)
        else:
            total = sum_x[h - 1, :, z].astype(F32)
            for d in range(nz - 1):
                total = total + sum_z[h - 1, d].astype(F32)
        sum_y[h] = total.astype(BF16)
        on_y[h] = start([remote(sum_y.at[h, 1 - y_hi], from_y.at[h], far)])[0]

    def last(h):
        on_y[h].wait_recv()
        total = sum_y[h, y_hi].astype(F32) + from_y[h].astype(F32)
        gqkv_ref[:, 192 * h : 192 * h + 192] = total[:, 0:192]
        gout_ref[:, 64 * h : 64 * h + 64] = total[:, 192:256]

    for h in range(4):
        for w in range(2):
            attend(w, h)
        if h < 3:
            weight(h)
            leave(h)

    def sum_heads(lv):
        att_l = dot(level_ref[lv], att[...]).astype(BF16)
        dqkv_l = dot(level_ref[lv], dqkv[...]).astype(BF16)
        term[lv, 0] = dot(att_l, wout_ref[...]).astype(BF16)
        term[lv, 1] = dot(dqkv_l, wqkv_ref[...], 1, 1).astype(BF16)

    chunks = [(at, CHUNK) for at in range(0, T_ROWS, CHUNK)]
    sum_heads(1 - core)
    on_core = start([
        remote(term.at[1 - core, :, pl.ds(at, size)], from_core.at[:, pl.ds(at, size)], sibling) for at, size in chunks
    ])
    sum_heads(core)
    on_side = []
    for copy, (at, size) in zip(on_core, chunks):
        copy.wait_recv()
        rows = pl.ds(at, size)
        to_side[rows] = (term[core, 1 - kind, rows].astype(F32) + from_core[1 - kind, rows].astype(F32)).astype(BF16)
        on_side += start([remote(to_side.at[rows], from_side.at[rows], side)])
    weight(3)
    tok_l[...] = dot(level_ref[core], tokc[...])
    cot_l[...] = dot(level_ref[core], cotc[...])

    def finish(chunk):
        rows = pl.ds(*chunks[chunk])
        on_side[chunk].wait_recv()
        total = term[core, kind, rows].astype(F32) + from_core[kind, rows].astype(F32) + from_side[rows].astype(F32)

        @pl.when(kind == 0)
        def _():
            result[rows] = (tok_l[rows] + total).astype(BF16)

        @pl.when(kind == 1)
        def _():
            scaled, inverse = layer_norm(tok_l[rows])
            grad = total * gain_ref[...]
            mean_grad = jnp.mean(grad, axis=-1, keepdims=True)
            mean_mixed = jnp.mean(grad * scaled, axis=-1, keepdims=True)
            result[rows] = (cot_l[rows] + (grad - mean_grad - scaled * mean_mixed) * inverse).astype(BF16)

    def share(chunk):
        rows = pl.ds(*chunks[chunk])
        return start([
            remote(final.at[kind, core, rows], final.at[kind, core, rows], side),
            remote(final.at[kind, core, rows], final.at[kind, core, rows], sibling),
        ])

    def relay(chunk, copy):
        rows = pl.ds(*chunks[chunk])
        copy.wait_recv()
        return start([remote(final.at[1 - kind, core, rows], final.at[1 - kind, core, rows], sibling)])[0]

    def place(k, lv):
        field = dot(natural_ref[...], final[k, lv]).astype(BF16)

        @pl.when(k == 0)
        def _():
            layer_ref[lv] = field

        @pl.when(k == 1)
        def _():
            dtok_ref[lv] = field

    first, middle, end = (pl.ds(*chunk) for chunk in chunks)
    finish(0)
    straight = start([remote(result.at[first], final.at[kind, core, first], {"lat": lat_up})])[0]
    second(1)
    finish(1)
    spread_out[...] = dot(spread_ref[...], result[middle]).astype(BF16)
    returned = start([
        remote(spread_out.at[pl.ds(at, size)], back.at[pl.ds(at, size)], target)
        for at, size, target in ((0, 16, {"lat": lat_up}), (16, 32, {"lon": lon_up}), (48, 32, {"lat": lat_up, "lon": lon_up}))
    ])
    leave(3)
    finish(2)
    final[kind, core, end] = result[end]
    shared = {2: share(2)}
    straight.wait_recv()
    shared[0] = share(0)
    second(0)
    second(2)
    third(1)
    for copy in returned:
        copy.wait_recv()
    back[U_ROWS : U_ROWS + CHUNK] = result[middle]
    final[kind, core, middle] = dot(gather_ref[...], back[...]).astype(BF16)
    shared[1] = share(1)
    place(kind, core)
    relayed = [relay(2, shared[2][0]), relay(0, shared[0][0])]
    third(2)
    third(0)
    second(3)
    relayed.append(relay(1, shared[1][0]))
    place(1 - kind, core)
    last(1)
    for chunk in range(3):
        shared[chunk][1].wait_recv()
    place(kind, 1 - core)
    third(3)
    for copy in relayed:
        copy.wait_recv()
    place(1 - kind, 1 - core)
    last(0)
    last(2)
    last(3)
    for copy in started:
        copy.wait_send()


def body(tokens, norm_gain, w_qkv, w_out, bias_table, cotangent):
    nlon, nlat = lax.axis_size("lon"), lax.axis_size("lat")
    nz = nlon // 2
    width = tokens.shape[-1]
    rows = width // (nlon * nlat)
    half = CELLS // LEV
    vmem = pl.BlockSpec(memory_space=pltpu.VMEM)
    hbm = pl.BlockSpec(memory_space=pl.ANY)
    copies = 4 + 4 + 4 * (nlat - 1 + nz - 1 + 1) + 3 + 3 + 4 + 9
    shape = lambda *dims: pltpu.VMEM(dims, BF16)
    own, compact, level, spread, gather, natural, select, eye, cross = [jnp.asarray(t) for t in tables()]
    operands = (
        tokens.reshape(CELLS, width), cotangent.reshape(CELLS, width), own, bias_table.T, select, cross, compact,
        norm_gain.reshape(1, width), w_qkv, w_out, eye, level, spread, gather, natural,
    )
    layer, dtok, gqkv, gout = pl.pallas_call(
        functools.partial(kernel, nlon, nlat),
        out_shape=(shape(LEV, half, width), shape(LEV, half, width), pltpu.VMEM((rows, 768), F32), pltpu.VMEM((rows, 256), F32)),
        in_specs=[hbm] * 15,
        out_specs=(vmem,) * 4,
        scratch_shapes=[
            shape(2, G_ROWS - 112, width),
            shape(2, G_ROWS, width),
            shape(CELLS, width),
            shape(CELLS, width),
            shape(CELLS, width),
            shape(width, CELLS),
            shape(width, CELLS),
            shape(CELLS, 768),
            shape(CELLS, 256),
            pltpu.VMEM((8, 768), F32),
            pltpu.VMEM((WINDOW, SEL), F32),
            pltpu.VMEM((4, WINDOW, WINDOW), F32),
            shape(CELLS, 768),
            shape(CELLS, 256),
            shape(4, 2, nz, nlat, rows, 256),
            shape(3, nlat - 1, 2, nz, rows, 256),
            shape(3, 2, nz, rows, 256),
            shape(max(nz - 1, 1), 2, nlat, rows, 256),
            shape(2, nlat, rows, 256),
            shape(3, max(nz - 1, 1), 2, rows, 256),
            shape(nlat - 1, 2, rows, 256),
            shape(4, 2, rows, 256),
            shape(4, rows, 256),
            shape(LEV, 2, T_ROWS, width),
            shape(2, T_ROWS, width),
            shape(T_ROWS, width),
            shape(T_ROWS, width),
            pltpu.VMEM((T_ROWS, width), F32),
            pltpu.VMEM((T_ROWS, width), F32),
            shape(T_ROWS, width),
            shape(U_ROWS, width),
            shape(U_ROWS + CHUNK, width),
            shape(2, LEV, T_ROWS, width),
            *[pltpu.VMEM(x.shape, x.dtype) for x in operands],
            pltpu.SemaphoreType.DMA((copies,)),
            pltpu.SemaphoreType.DMA((copies,)),
            pltpu.SemaphoreType.DMA((len(operands),)),
        ],
        compiler_params=pltpu.CompilerParams(
            collective_id=0, has_side_effects=True, vmem_limit_bytes=56 * 1024 * 1024
        ),
    )(*operands)
    field = (LEV, WLAT, LON, width)
    return layer.reshape(field), dtok.reshape(field), gqkv, gout.T


def solution(mesh):
    in_specs = (
        P(None, "lat", "lon", None),
        P(),
        P(None, "head"),
        P("head", None),
        P(None, "head"),
        P(None, "lat", "lon", None),
    )
    out_specs = (
        P(None, "lat", "lon", None),
        P(None, "lat", "lon", None),
        P(("lon", "lat"), "head"),
        P("head", ("lon", "lat")),
    )
    return jax.shard_map(body, mesh=mesh, in_specs=in_specs, out_specs=out_specs, check_vma=False)
```

```python
import functools

import jax
import jax.numpy as jnp
import ml_dtypes
import numpy as np
from jax import lax
from jax.experimental import pallas as pl
from jax.experimental.pallas import tpu as pltpu
from jax.sharding import PartitionSpec as P

MESH = pl.DeviceIdType.MESH
HEAD_DIM = 64
LEV = 2
WLAT = 6
WLON = 12
LON = 24
WINDOW = LEV * WLAT * WLON
CELLS = LEV * WLAT * LON
EPSILON = 1e-05
NEG_FILL = -1e30
F32 = jnp.float32
BF16 = jnp.bfloat16

G_START = (0, 112, 224, 272)
G_ROWS = 320
T_START = (90, 0, 54, 72)
T_ROWS = 144
CHUNK = 48
U_START = (None, 0, 16, 48)
U_ROWS = 80
SEL = 384


def quarter(row, col):
    down, right = row >= 3, col >= 18
    part = (2 if right else 0) + (1 if down else 0)
    width = 6 if right else 18
    return part, (row % 3) * width + (col - 18 if right else col), 3 * width


def tables():
    own = np.zeros((G_ROWS, CELLS), np.float32)
    compact = np.zeros((CELLS, G_ROWS), np.float32)
    level = np.zeros((LEV, T_ROWS, CELLS), np.float32)
    spread = np.zeros((U_ROWS, CHUNK), np.float32)
    gather = np.zeros((CHUNK, U_ROWS + CHUNK), np.float32)
    natural = np.zeros((CELLS // LEV, T_ROWS), np.float32)
    for lv in range(LEV):
        for row in range(WLAT):
            for col in range(LON):
                part, index, size = quarter(row, col)
                held = G_START[part] + lv * size + index
                src_row = row + 3 if row < 3 else row - 3
                src_col = col + 6 if col < 18 else col - 18
                own[held, lv * 144 + src_row * LON + src_col] = 1
                place = (col // WLON) * WINDOW + lv * 72 + row * WLON + col % WLON
                compact[place, held] = 1
                level[lv, T_START[part] + index, place] = 1
                if lv == 0:
                    natural[src_row * LON + src_col, T_START[part] + index] = 1
                    at = T_START[part] + index - CHUNK
                    if 0 <= at < CHUNK and part:
                        travel = U_START[part] + (at if part == 1 else index)
                        spread[travel, at] = 1
                        gather[at, travel] = 1
                    elif 0 <= at < CHUNK:
                        gather[at, U_ROWS + at] = 1
    select = np.zeros((SEL, WINDOW), np.float32)
    for i in range(WINDOW):
        select[(i // 72) * 253 + (i // WLON % WLAT) * 23 + i % WLON, i] = 1
    half = np.arange(WINDOW) // WLON % WLAT >= 3
    cross = (half[:, None] != half[None, :]).astype(np.float32)
    exact = [t.astype(ml_dtypes.bfloat16) for t in (own, compact, level, spread, gather, natural, select, np.eye(128, dtype=np.float32))]
    return exact + [cross]


def dot(a, b, ca=1, cb=0):
    return lax.dot_general(a, b, (((ca,), (cb,)), ((), ())), preferred_element_type=F32)


def layer_norm(floats):
    center = floats - jnp.mean(floats, axis=-1, keepdims=True)
    inverse = lax.rsqrt(jnp.mean(center * center, axis=-1, keepdims=True) + EPSILON)
    return center * inverse, inverse


def kernel(
    nlon, nlat,
    tok_in, cot_in, own_in, table_in, select_in, cross_in, compact_in, gain_in, wqkv_in, wout_in, eye_in,
    level_in, spread_in, gather_in, natural_in,
    layer_ref, dtok_ref, gqkv_ref, gout_ref,
    sent, held, tokc, cotc, normed, normed_t, cot_t, qkv, datt, wide_table, rolled, bias, dqkv, att,
    wgt, relay_up, relay_down, added_up, added_down, from_below, from_above, sum_x, from_lon,
    near_z, first_z, last_x, sum_y, from_y,
    term, from_core, to_side, from_side, tok_l, cot_l, result, spread_out, back, final,
    tok_ref, cot_ref, own_ref, table_ref, select_ref, cross_ref, compact_ref, gain_ref, wqkv_ref, wout_ref, eye_ref,
    level_ref, spread_ref, gather_ref, natural_ref,
    send_sem, recv_sem, in_sem,
):
    lon, lat, head = lax.axis_index("lon"), lax.axis_index("lat"), lax.axis_index("head")
    nz = nlon // 2
    y_hi, z = lon // nz, lon % nz
    kind, core = head // 2, head % 2
    lat_up, lat_down = (lat + 1) % nlat, (lat + nlat - 1) % nlat
    lon_up, lon_down = (lon + 1) % nlon, (lon + nlon - 1) % nlon
    sibling = {"head": kind * 2 + 1 - core}
    side = {"head": (1 - kind) * 2 + core}
    x_up = [{"lat": (lat + d) % nlat} for d in range(1, nlat)]
    x_down = [{"lat": (lat + nlat - d) % nlat} for d in range(1, nlat)]
    z_up = [{"lon": y_hi * nz + (z + d) % nz} for d in range(1, nz)]
    z_down = [{"lon": y_hi * nz + (z + nz - d) % nz} for d in range(1, nz)]
    far = {"lon": (1 - y_hi) * nz + z}

    lon_others = [{"lon": (lon + d) % nlon} for d in range(1, nlon)]
    opposite = (lat + 2) % nlat

    sources = x_down + lon_others + [
        sibling, side,
        {"lat": lat_up, "lon": lon_up}, {"lat": lat_down, "lon": lon_down},
    ]
    barrier = pltpu.get_barrier_semaphore()
    for source in sources:
        pl.semaphore_signal(barrier, inc=1, device_id=source, device_id_type=MESH)

    loads = [
        pltpu.make_async_copy(src, dst, in_sem.at[i])
        for i, (src, dst) in enumerate((
            (tok_in, tok_ref), (cot_in, cot_ref), (own_in, own_ref), (table_in, table_ref), (select_in, select_ref),
            (cross_in, cross_ref), (compact_in, compact_ref), (gain_in, gain_ref), (wqkv_in, wqkv_ref), (wout_in, wout_ref),
            (eye_in, eye_ref), (level_in, level_ref), (spread_in, spread_ref), (gather_in, gather_ref), (natural_in, natural_ref),
        ))
    ]
    for load in loads:
        load.start()
    for load in loads[:3]:
        load.wait()

    count = [0]

    def remote(src, dst, target):
        index = count[0]
        count[0] += 1
        return pltpu.make_async_remote_copy(
            src_ref=src, dst_ref=dst, send_sem=send_sem.at[index], recv_sem=recv_sem.at[index],
            device_id=target, device_id_type=MESH,
        )

    started = []

    def start(copies):
        for copy in copies:
            copy.start()
        started.extend(copies)
        return copies

    for i, ref in enumerate((tok_ref, cot_ref)):
        arranged = dot(own_ref[...], ref[...]).astype(BF16)
        held[i, 0:112] = arranged[0:112]
        sent[i] = arranged[112:]
    pl.semaphore_wait(barrier, len(sources))
    diagonal = {"lat": lat_down, "lon": lon_down}
    parts = [(112, 64, {"lat": lat_down}), (224, 48, {"lon": lon_down}), (272, 48, diagonal), (176, 48, {"lat": lat_down})]
    shifted = start([
        remote(sent.at[core, pl.ds(at - 112, size)], held.at[core, pl.ds(at, size)], target) for at, size, target in parts
    ])

    for load in loads[3:]:
        load.wait()

    wide_table[...] = jnp.zeros(wide_table.shape, F32)
    wide_table[0:4, 0 : table_ref.shape[1]] = table_ref[...]
    turned = wide_table[...]
    for h in range(4):
        stepped = jnp.broadcast_to(turned[h : h + 1, :], (16, turned.shape[1]))
        stepped = pltpu.roll(stepped, 0, 1, stride=1, stride_axis=0)
        for step in range(LEV * WLAT):
            offset = (step // WLAT) * 253 + (step % WLAT) * 23
            shift = (offset - 379) % turned.shape[1]
            moved = pltpu.roll(stepped, shift, 1)
            rolled[WLON * step : WLON * step + WLON, :] = moved[0:WLON, 0:SEL]
        rest = rolled[...]
        total = jnp.zeros((WINDOW, WINDOW), F32)
        for _ in range(3):
            piece = rest.astype(BF16)
            rest = rest - piece.astype(F32)
            total = total + dot(piece, select_ref[...])
        excluded = (cross_ref[...] > 0.5) & (lat == nlat - 1)
        bias[h] = jnp.where(excluded, NEG_FILL, total)

    forwards = []
    for copy, (at, size, _) in zip(shifted, parts):
        copy.wait_recv()
        forwards += start([remote(held.at[core, pl.ds(at, size)], held.at[core, pl.ds(at, size)], sibling)])
    for copy in forwards:
        copy.wait_recv()

    tokc[...] = dot(compact_ref[...], held[0]).astype(BF16)
    cotc[...] = dot(compact_ref[...], held[1]).astype(BF16)
    for at in range(0, CELLS, 48):
        scaled, _ = layer_norm(tokc[at : at + 48, :].astype(F32))
        normed[at : at + 48, :] = (scaled * gain_ref[...]).astype(BF16)
    qkv[...] = dot(normed[...], wqkv_ref[...]).astype(BF16)
    datt[...] = dot(cotc[...], wout_ref[...], 1, 1).astype(BF16)
    for at in range(0, normed.shape[1], 128):
        normed_t[at : at + 128, :] = dot(eye_ref[...], normed[:, at : at + 128], 1, 1).astype(BF16)
        cot_t[at : at + 128, :] = dot(eye_ref[...], cotc[:, at : at + 128], 1, 1).astype(BF16)

    def attend(w, h):
        rows = pl.ds(w * WINDOW, WINDOW)
        first = 3 * HEAD_DIM * h
        query = qkv[rows, first : first + 64]
        key = qkv[rows, first + 64 : first + 128]
        value = qkv[rows, first + 128 : first + 192]
        grad = datt[rows, 64 * h : 64 * h + 64]
        scores = dot(key, query, 1, 1) * (HEAD_DIM ** -0.5) + bias[h]
        raised = jnp.exp(scores - jnp.max(scores, axis=0, keepdims=True))
        prob = raised * (1.0 / jnp.sum(raised, axis=0, keepdims=True))
        half = prob.astype(BF16)
        grad_prob = dot(value, grad, 1, 1)
        row_term = jnp.sum(prob * grad_prob, axis=0, keepdims=True)
        grad_score = (prob * (grad_prob - row_term) * (HEAD_DIM ** -0.5)).astype(BF16)
        att[rows, 64 * h : 64 * h + 64] = dot(half, value, 0, 0).astype(BF16)
        dqkv[rows, first : first + 64] = dot(grad_score, key, 0, 0).astype(BF16)
        dqkv[rows, first + 64 : first + 128] = dot(grad_score, query, 1, 0).astype(BF16)
        dqkv[rows, first + 128 : first + 192] = dot(half, grad, 1, 0).astype(BF16)

    rows_out = wgt.shape[4]
    on_relay, on_first, on_second, on_y = {}, {}, {}, {}
    low, high = pl.ds(0, 128), pl.ds(128, 128)

    def weight(h):
        wide = dot(normed_t[...], dqkv[:, 192 * h : 192 * h + 192]).astype(BF16)
        wgt[h, :, :, :, :, 0:192] = wide.reshape(2, nz, nlat, rows_out, 192)
        narrow = dot(cot_t[...], att[:, 64 * h : 64 * h + 64]).astype(BF16)
        wgt[h, :, :, :, :, 192:256] = narrow.reshape(2, nz, nlat, rows_out, 64)

    def leave(h):
        if h == 0:
            on_first[h] = start([
                remote(wgt.at[h, :, target["lon"] - y_hi * nz], near_z.at[d], target) for d, target in enumerate(z_up)
            ])
        else:
            up, down = {"lat": lat_up}, {"lat": lat_down}
            on_relay[h] = start([
                remote(wgt.at[h, :, :, opposite, :, low], relay_up.at[h - 1], up),
                remote(wgt.at[h, :, :, opposite, :, high], relay_down.at[h - 1], down),
            ])
            on_first[h] = start([
                remote(wgt.at[h, :, :, lat_up, :, high], from_below.at[h - 1, :, :, :, high], up),
                remote(wgt.at[h, :, :, lat_down, :, low], from_above.at[h - 1, :, :, :, low], down),
            ])

    def onward(h):
        up, down = {"lat": lat_up}, {"lat": lat_down}
        for copy in on_relay[h]:
            copy.wait_recv()
        added_up[h - 1] = (wgt[h, :, :, lat_up, :, low].astype(F32) + relay_up[h - 1].astype(F32)).astype(BF16)
        added_down[h - 1] = (wgt[h, :, :, lat_down, :, high].astype(F32) + relay_down[h - 1].astype(F32)).astype(BF16)
        on_first[h] += start([
            remote(added_up.at[h - 1], from_below.at[h - 1, :, :, :, low], up),
            remote(added_down.at[h - 1], from_above.at[h - 1, :, :, :, high], down),
        ])

    def second(h):
        for copy in on_first[h]:
            copy.wait_recv()
        if h == 0:
            total = wgt[h, :, z].astype(F32)
            for d in range(nz - 1):
                total = total + near_z[d].astype(F32)
            first_z[...] = total.astype(BF16)
            on_second[h] = start([
                remote(first_z.at[:, target["lat"]], last_x.at[d], target) for d, target in enumerate(x_up)
            ])
        else:
            total = wgt[h, :, :, lat].astype(F32) + from_below[h - 1].astype(F32) + from_above[h - 1].astype(F32)
            sum_x[h - 1] = total.astype(BF16).reshape(sum_x.shape[1:])
            on_second[h] = start([
                remote(sum_x.at[h - 1, target["lon"]], from_lon.at[h - 1, d], target) for d, target in enumerate(lon_others)
            ])

    def third(h):
        for copy in on_second[h]:
            copy.wait_recv()
        total = first_z[:, lat].astype(F32)
        for d in range(nlat - 1):
            total = total + last_x[d].astype(F32)
        sum_y[...] = total.astype(BF16)
        on_y[h] = start([remote(sum_y.at[1 - y_hi], from_y, far)])[0]

    def last(h):
        if h == 0:
            on_y[h].wait_recv()
            total = sum_y[y_hi].astype(F32) + from_y[...].astype(F32)
        else:
            for copy in on_second[h]:
                copy.wait_recv()
            total = sum_x[h - 1, lon].astype(F32)
            for d in range(nlon - 1):
                total = total + from_lon[h - 1, d].astype(F32)
        gqkv_ref[:, 192 * h : 192 * h + 192] = total[:, 0:192]
        gout_ref[:, 64 * h : 64 * h + 64] = total[:, 192:256]

    for h in range(4):
        for w in range(2):
            attend(w, h)
        if h < 3:
            weight(h)
            leave(h)

    def sum_heads(lv):
        att_l = dot(level_ref[lv], att[...]).astype(BF16)
        dqkv_l = dot(level_ref[lv], dqkv[...]).astype(BF16)
        term[lv, 0] = dot(att_l, wout_ref[...]).astype(BF16)
        term[lv, 1] = dot(dqkv_l, wqkv_ref[...], 1, 1).astype(BF16)

    chunks = [(at, CHUNK) for at in range(0, T_ROWS, CHUNK)]
    sum_heads(1 - core)
    on_core = start([
        remote(term.at[1 - core, :, pl.ds(at, size)], from_core.at[:, pl.ds(at, size)], sibling) for at, size in chunks
    ])
    sum_heads(core)
    on_side = []
    for copy, (at, size) in zip(on_core, chunks):
        copy.wait_recv()
        rows = pl.ds(at, size)
        to_side[rows] = (term[core, 1 - kind, rows].astype(F32) + from_core[1 - kind, rows].astype(F32)).astype(BF16)
        on_side += start([remote(to_side.at[rows], from_side.at[rows], side)])
    onward(1)
    weight(3)
    leave(3)
    onward(2)
    tok_l[...] = dot(level_ref[core], tokc[...])
    cot_l[...] = dot(level_ref[core], cotc[...])

    def finish(chunk):
        rows = pl.ds(*chunks[chunk])
        on_side[chunk].wait_recv()
        total = term[core, kind, rows].astype(F32) + from_core[kind, rows].astype(F32) + from_side[rows].astype(F32)

        @pl.when(kind == 0)
        def _():
            result[rows] = (tok_l[rows] + total).astype(BF16)

        @pl.when(kind == 1)
        def _():
            scaled, inverse = layer_norm(tok_l[rows])
            grad = total * gain_ref[...]
            mean_grad = jnp.mean(grad, axis=-1, keepdims=True)
            mean_mixed = jnp.mean(grad * scaled, axis=-1, keepdims=True)
            result[rows] = (cot_l[rows] + (grad - mean_grad - scaled * mean_mixed) * inverse).astype(BF16)

    def share(chunk):
        rows = pl.ds(*chunks[chunk])
        return start([
            remote(final.at[kind, core, rows], final.at[kind, core, rows], side),
            remote(final.at[kind, core, rows], final.at[kind, core, rows], sibling),
        ])

    def relay(chunk, copy):
        rows = pl.ds(*chunks[chunk])
        copy.wait_recv()
        return start([remote(final.at[1 - kind, core, rows], final.at[1 - kind, core, rows], sibling)])[0]

    def place(k, lv):
        field = dot(natural_ref[...], final[k, lv]).astype(BF16)

        @pl.when(k == 0)
        def _():
            layer_ref[lv] = field

        @pl.when(k == 1)
        def _():
            dtok_ref[lv] = field

    first, middle, end = (pl.ds(*chunk) for chunk in chunks)
    finish(0)
    straight = start([remote(result.at[first], final.at[kind, core, first], {"lat": lat_up})])[0]
    finish(1)
    spread_out[...] = dot(spread_ref[...], result[middle]).astype(BF16)
    returned = start([
        remote(spread_out.at[pl.ds(at, size)], back.at[pl.ds(at, size)], target)
        for at, size, target in ((0, 16, {"lat": lat_up}), (16, 32, {"lon": lon_up}), (48, 32, {"lat": lat_up, "lon": lon_up}))
    ])
    second(1)
    finish(2)
    onward(3)
    final[kind, core, end] = result[end]
    shared = {2: share(2)}
    straight.wait_recv()
    shared[0] = share(0)
    second(0)
    second(2)
    for copy in returned:
        copy.wait_recv()
    back[U_ROWS : U_ROWS + CHUNK] = result[middle]
    final[kind, core, middle] = dot(gather_ref[...], back[...]).astype(BF16)
    shared[1] = share(1)
    place(kind, core)
    relayed = [relay(2, shared[2][0]), relay(0, shared[0][0])]
    third(0)
    second(3)
    relayed.append(relay(1, shared[1][0]))
    place(1 - kind, core)
    last(1)
    for chunk in range(3):
        shared[chunk][1].wait_recv()
    place(kind, 1 - core)
    for copy in relayed:
        copy.wait_recv()
    place(1 - kind, 1 - core)
    last(0)
    last(2)
    last(3)
    for copy in started:
        copy.wait_send()


def body(tokens, norm_gain, w_qkv, w_out, bias_table, cotangent):
    nlon, nlat = lax.axis_size("lon"), lax.axis_size("lat")
    nz = nlon // 2
    width = tokens.shape[-1]
    rows = width // (nlon * nlat)
    half = CELLS // LEV
    vmem = pl.BlockSpec(memory_space=pltpu.VMEM)
    hbm = pl.BlockSpec(memory_space=pl.ANY)
    copies = 4 + 4 + (nlat - 1 + nz - 1 + 1) + 3 * (6 + nlon - 1) + 3 + 3 + 4 + 9
    shape = lambda *dims: pltpu.VMEM(dims, BF16)
    own, compact, level, spread, gather, natural, select, eye, cross = [jnp.asarray(t) for t in tables()]
    operands = (
        tokens.reshape(CELLS, width), cotangent.reshape(CELLS, width), own, bias_table.T, select, cross, compact,
        norm_gain.reshape(1, width), w_qkv, w_out, eye, level, spread, gather, natural,
    )
    layer, dtok, gqkv, gout = pl.pallas_call(
        functools.partial(kernel, nlon, nlat),
        out_shape=(shape(LEV, half, width), shape(LEV, half, width), pltpu.VMEM((rows, 768), F32), pltpu.VMEM((rows, 256), F32)),
        in_specs=[hbm] * 15,
        out_specs=(vmem,) * 4,
        scratch_shapes=[
            shape(2, G_ROWS - 112, width),
            shape(2, G_ROWS, width),
            shape(CELLS, width),
            shape(CELLS, width),
            shape(CELLS, width),
            shape(width, CELLS),
            shape(width, CELLS),
            shape(CELLS, 768),
            shape(CELLS, 256),
            pltpu.VMEM((8, 768), F32),
            pltpu.VMEM((WINDOW, SEL), F32),
            pltpu.VMEM((4, WINDOW, WINDOW), F32),
            shape(CELLS, 768),
            shape(CELLS, 256),
            shape(4, 2, nz, nlat, rows, 256),
            *[shape(3, 2, nz, rows, 128)] * 4,
            *[shape(3, 2, nz, rows, 256)] * 2,
            shape(3, nlon, rows, 256),
            shape(3, nlon - 1, rows, 256),
            shape(max(nz - 1, 1), 2, nlat, rows, 256),
            shape(2, nlat, rows, 256),
            shape(nlat - 1, 2, rows, 256),
            shape(2, rows, 256),
            shape(rows, 256),
            shape(LEV, 2, T_ROWS, width),
            shape(2, T_ROWS, width),
            shape(T_ROWS, width),
            shape(T_ROWS, width),
            pltpu.VMEM((T_ROWS, width), F32),
            pltpu.VMEM((T_ROWS, width), F32),
            shape(T_ROWS, width),
            shape(U_ROWS, width),
            shape(U_ROWS + CHUNK, width),
            shape(2, LEV, T_ROWS, width),
            *[pltpu.VMEM(x.shape, x.dtype) for x in operands],
            pltpu.SemaphoreType.DMA((copies,)),
            pltpu.SemaphoreType.DMA((copies,)),
            pltpu.SemaphoreType.DMA((len(operands),)),
        ],
        compiler_params=pltpu.CompilerParams(
            collective_id=0, has_side_effects=True, vmem_limit_bytes=56 * 1024 * 1024
        ),
    )(*operands)
    field = (LEV, WLAT, LON, width)
    return layer.reshape(field), dtok.reshape(field), gqkv, gout.T


def solution(mesh):
    in_specs = (
        P(None, "lat", "lon", None),
        P(),
        P(None, "head"),
        P("head", None),
        P(None, "head"),
        P(None, "lat", "lon", None),
    )
    out_specs = (
        P(None, "lat", "lon", None),
        P(None, "lat", "lon", None),
        P(("lon", "lat"), "head"),
        P("head", ("lon", "lat")),
    )
    return jax.shard_map(body, mesh=mesh, in_specs=in_specs, out_specs=out_specs, check_vma=False)
```

```python
import functools

import jax
import jax.numpy as jnp
import ml_dtypes
import numpy as np
from jax import lax
from jax.experimental import pallas as pl
from jax.experimental.pallas import tpu as pltpu
from jax.sharding import PartitionSpec as P

MESH = pl.DeviceIdType.MESH
HEAD_DIM = 64
LEV = 2
WLAT = 6
WLON = 12
LON = 24
WINDOW = LEV * WLAT * WLON
CELLS = LEV * WLAT * LON
EPSILON = 1e-05
NEG_FILL = -1e30
F32 = jnp.float32
BF16 = jnp.bfloat16

G_START = (0, 112, 224, 272)
G_ROWS = 320
T_START = (90, 0, 54, 72)
T_ROWS = 144
CHUNK = 48
U_START = (None, 0, 16, 48)
U_ROWS = 80
SEL = 384


def quarter(row, col):
    down, right = row >= 3, col >= 18
    part = (2 if right else 0) + (1 if down else 0)
    width = 6 if right else 18
    return part, (row % 3) * width + (col - 18 if right else col), 3 * width


def tables():
    own = np.zeros((G_ROWS, CELLS), np.float32)
    compact = np.zeros((CELLS, G_ROWS), np.float32)
    level = np.zeros((LEV, T_ROWS, CELLS), np.float32)
    spread = np.zeros((U_ROWS, CHUNK), np.float32)
    gather = np.zeros((CHUNK, U_ROWS + CHUNK), np.float32)
    natural = np.zeros((CELLS // LEV, T_ROWS), np.float32)
    for lv in range(LEV):
        for row in range(WLAT):
            for col in range(LON):
                part, index, size = quarter(row, col)
                held = G_START[part] + lv * size + index
                src_row = row + 3 if row < 3 else row - 3
                src_col = col + 6 if col < 18 else col - 18
                own[held, lv * 144 + src_row * LON + src_col] = 1
                place = (col // WLON) * WINDOW + lv * 72 + row * WLON + col % WLON
                compact[place, held] = 1
                level[lv, T_START[part] + index, place] = 1
                if lv == 0:
                    natural[src_row * LON + src_col, T_START[part] + index] = 1
                    at = T_START[part] + index - CHUNK
                    if 0 <= at < CHUNK and part:
                        travel = U_START[part] + (at if part == 1 else index)
                        spread[travel, at] = 1
                        gather[at, travel] = 1
                    elif 0 <= at < CHUNK:
                        gather[at, U_ROWS + at] = 1
    select = np.zeros((SEL, WINDOW), np.float32)
    for i in range(WINDOW):
        select[(i // 72) * 253 + (i // WLON % WLAT) * 23 + i % WLON, i] = 1
    half = np.arange(WINDOW) // WLON % WLAT >= 3
    cross = (half[:, None] != half[None, :]).astype(np.float32)
    exact = [t.astype(ml_dtypes.bfloat16) for t in (own, compact, level, spread, gather, natural, select, np.eye(128, dtype=np.float32))]
    return exact + [cross]


def dot(a, b, ca=1, cb=0):
    return lax.dot_general(a, b, (((ca,), (cb,)), ((), ())), preferred_element_type=F32)


def layer_norm(floats):
    center = floats - jnp.mean(floats, axis=-1, keepdims=True)
    inverse = lax.rsqrt(jnp.mean(center * center, axis=-1, keepdims=True) + EPSILON)
    return center * inverse, inverse


def kernel(
    nlon, nlat,
    tok_in, cot_in, own_in, table_in, select_in, cross_in, compact_in, gain_in, wqkv_in, wout_in, eye_in,
    level_in, spread_in, gather_in, natural_in,
    layer_ref, dtok_ref, gqkv_ref, gout_ref,
    sent, held, tokc, cotc, normed, normed_t, cot_t, qkv, datt, wide_table, rolled, bias, dqkv, att,
    wgt, relay_up, relay_down, added_up, added_down, from_below, from_above, sum_x, rows_far, sum_far, from_far, sum_z, from_z,
    near_z, first_z, last_x, sum_y, from_y,
    term, from_core, to_side, from_side, tok_l, cot_l, result, spread_out, back, final,
    tok_ref, cot_ref, own_ref, table_ref, select_ref, cross_ref, compact_ref, gain_ref, wqkv_ref, wout_ref, eye_ref,
    level_ref, spread_ref, gather_ref, natural_ref,
    send_sem, recv_sem, in_sem,
):
    lon, lat, head = lax.axis_index("lon"), lax.axis_index("lat"), lax.axis_index("head")
    nz = nlon // 2
    y_hi, z = lon // nz, lon % nz
    kind, core = head // 2, head % 2
    lat_up, lat_down = (lat + 1) % nlat, (lat + nlat - 1) % nlat
    lon_up, lon_down = (lon + 1) % nlon, (lon + nlon - 1) % nlon
    sibling = {"head": kind * 2 + 1 - core}
    side = {"head": (1 - kind) * 2 + core}
    x_up = [{"lat": (lat + d) % nlat} for d in range(1, nlat)]
    x_down = [{"lat": (lat + nlat - d) % nlat} for d in range(1, nlat)]
    z_up = [{"lon": y_hi * nz + (z + d) % nz} for d in range(1, nz)]
    z_down = [{"lon": y_hi * nz + (z + nz - d) % nz} for d in range(1, nz)]
    far = {"lon": (1 - y_hi) * nz + z}

    opposite = (lat + 2) % nlat

    sources = x_down + z_down + [
        far, sibling, side, {"lon": lon_up}, {"lon": lon_down},
        {"lat": lat_up, "lon": lon_up}, {"lat": lat_down, "lon": lon_down},
    ]
    barrier = pltpu.get_barrier_semaphore()
    for source in sources:
        pl.semaphore_signal(barrier, inc=1, device_id=source, device_id_type=MESH)

    loads = [
        pltpu.make_async_copy(src, dst, in_sem.at[i])
        for i, (src, dst) in enumerate((
            (tok_in, tok_ref), (cot_in, cot_ref), (own_in, own_ref), (table_in, table_ref), (select_in, select_ref),
            (cross_in, cross_ref), (compact_in, compact_ref), (gain_in, gain_ref), (wqkv_in, wqkv_ref), (wout_in, wout_ref),
            (eye_in, eye_ref), (level_in, level_ref), (spread_in, spread_ref), (gather_in, gather_ref), (natural_in, natural_ref),
        ))
    ]
    for load in loads:
        load.start()
    for load in loads[:3]:
        load.wait()

    count = [0]

    def remote(src, dst, target):
        index = count[0]
        count[0] += 1
        return pltpu.make_async_remote_copy(
            src_ref=src, dst_ref=dst, send_sem=send_sem.at[index], recv_sem=recv_sem.at[index],
            device_id=target, device_id_type=MESH,
        )

    started = []

    def start(copies):
        for copy in copies:
            copy.start()
        started.extend(copies)
        return copies

    for i, ref in enumerate((tok_ref, cot_ref)):
        arranged = dot(own_ref[...], ref[...]).astype(BF16)
        held[i, 0:112] = arranged[0:112]
        sent[i] = arranged[112:]
    pl.semaphore_wait(barrier, len(sources))
    diagonal = {"lat": lat_down, "lon": lon_down}
    parts = [(112, 64, {"lat": lat_down}), (224, 48, {"lon": lon_down}), (272, 48, diagonal), (176, 48, {"lat": lat_down})]
    shifted = start([
        remote(sent.at[core, pl.ds(at - 112, size)], held.at[core, pl.ds(at, size)], target) for at, size, target in parts
    ])

    for load in loads[3:]:
        load.wait()

    wide_table[...] = jnp.zeros(wide_table.shape, F32)
    wide_table[0:4, 0 : table_ref.shape[1]] = table_ref[...]
    turned = wide_table[...]
    for h in range(4):
        stepped = jnp.broadcast_to(turned[h : h + 1, :], (16, turned.shape[1]))
        stepped = pltpu.roll(stepped, 0, 1, stride=1, stride_axis=0)
        for step in range(LEV * WLAT):
            offset = (step // WLAT) * 253 + (step % WLAT) * 23
            shift = (offset - 379) % turned.shape[1]
            moved = pltpu.roll(stepped, shift, 1)
            rolled[WLON * step : WLON * step + WLON, :] = moved[0:WLON, 0:SEL]
        rest = rolled[...]
        total = jnp.zeros((WINDOW, WINDOW), F32)
        for _ in range(3):
            piece = rest.astype(BF16)
            rest = rest - piece.astype(F32)
            total = total + dot(piece, select_ref[...])
        excluded = (cross_ref[...] > 0.5) & (lat == nlat - 1)
        bias[h] = jnp.where(excluded, NEG_FILL, total)

    forwards = []
    for copy, (at, size, _) in zip(shifted, parts):
        copy.wait_recv()
        forwards += start([remote(held.at[core, pl.ds(at, size)], held.at[core, pl.ds(at, size)], sibling)])
    for copy in forwards:
        copy.wait_recv()

    tokc[...] = dot(compact_ref[...], held[0]).astype(BF16)
    cotc[...] = dot(compact_ref[...], held[1]).astype(BF16)
    for at in range(0, CELLS, 48):
        scaled, _ = layer_norm(tokc[at : at + 48, :].astype(F32))
        normed[at : at + 48, :] = (scaled * gain_ref[...]).astype(BF16)
    qkv[...] = dot(normed[...], wqkv_ref[...]).astype(BF16)
    datt[...] = dot(cotc[...], wout_ref[...], 1, 1).astype(BF16)
    for at in range(0, normed.shape[1], 128):
        normed_t[at : at + 128, :] = dot(eye_ref[...], normed[:, at : at + 128], 1, 1).astype(BF16)
        cot_t[at : at + 128, :] = dot(eye_ref[...], cotc[:, at : at + 128], 1, 1).astype(BF16)

    def attend(w, h):
        rows = pl.ds(w * WINDOW, WINDOW)
        first = 3 * HEAD_DIM * h
        query = qkv[rows, first : first + 64]
        key = qkv[rows, first + 64 : first + 128]
        value = qkv[rows, first + 128 : first + 192]
        grad = datt[rows, 64 * h : 64 * h + 64]
        scores = dot(key, query, 1, 1) * (HEAD_DIM ** -0.5) + bias[h]
        raised = jnp.exp(scores - jnp.max(scores, axis=0, keepdims=True))
        prob = raised * (1.0 / jnp.sum(raised, axis=0, keepdims=True))
        half = prob.astype(BF16)
        grad_prob = dot(value, grad, 1, 1)
        row_term = jnp.sum(prob * grad_prob, axis=0, keepdims=True)
        grad_score = (prob * (grad_prob - row_term) * (HEAD_DIM ** -0.5)).astype(BF16)
        att[rows, 64 * h : 64 * h + 64] = dot(half, value, 0, 0).astype(BF16)
        dqkv[rows, first : first + 64] = dot(grad_score, key, 0, 0).astype(BF16)
        dqkv[rows, first + 64 : first + 128] = dot(grad_score, query, 1, 0).astype(BF16)
        dqkv[rows, first + 128 : first + 192] = dot(half, grad, 1, 0).astype(BF16)

    rows_out = wgt.shape[4]
    far_first = (1,)
    on_relay, on_first, on_second, on_last, on_y = {}, {}, {}, {}, {}
    low, high = pl.ds(0, 128), pl.ds(128, 128)

    def weight(h):
        wide = dot(normed_t[...], dqkv[:, 192 * h : 192 * h + 192]).astype(BF16)
        wgt[h, :, :, :, :, 0:192] = wide.reshape(2, nz, nlat, rows_out, 192)
        narrow = dot(cot_t[...], att[:, 64 * h : 64 * h + 64]).astype(BF16)
        wgt[h, :, :, :, :, 192:256] = narrow.reshape(2, nz, nlat, rows_out, 64)

    def leave(h):
        if h == 0:
            on_first[h] = start([
                remote(wgt.at[h, :, target["lon"] - y_hi * nz], near_z.at[d], target) for d, target in enumerate(z_up)
            ])
        else:
            up, down = {"lat": lat_up}, {"lat": lat_down}
            on_relay[h] = start([
                remote(wgt.at[h, :, :, opposite, :, low], relay_up.at[h - 1], up),
                remote(wgt.at[h, :, :, opposite, :, high], relay_down.at[h - 1], down),
            ])
            on_first[h] = start([
                remote(wgt.at[h, :, :, lat_up, :, high], from_below.at[h - 1, :, :, :, high], up),
                remote(wgt.at[h, :, :, lat_down, :, low], from_above.at[h - 1, :, :, :, low], down),
            ])

    def onward(h):
        up, down = {"lat": lat_up}, {"lat": lat_down}
        for copy in on_relay[h]:
            copy.wait_recv()
        added_up[h - 1] = (wgt[h, :, :, lat_up, :, low].astype(F32) + relay_up[h - 1].astype(F32)).astype(BF16)
        added_down[h - 1] = (wgt[h, :, :, lat_down, :, high].astype(F32) + relay_down[h - 1].astype(F32)).astype(BF16)
        on_first[h] += start([
            remote(added_up.at[h - 1], from_below.at[h - 1, :, :, :, low], up),
            remote(added_down.at[h - 1], from_above.at[h - 1, :, :, :, high], down),
        ])

    def second(h):
        for copy in on_first[h]:
            copy.wait_recv()
        if h == 0:
            total = wgt[h, :, z].astype(F32)
            for d in range(nz - 1):
                total = total + near_z[d].astype(F32)
            first_z[...] = total.astype(BF16)
            on_second[h] = start([
                remote(first_z.at[:, target["lat"]], last_x.at[d], target) for d, target in enumerate(x_up)
            ])
        else:
            total = wgt[h, :, :, lat].astype(F32) + from_below[h - 1].astype(F32) + from_above[h - 1].astype(F32)
            sum_x[h - 1] = total.astype(BF16)
            if h in far_first:
                on_second[h] = start([remote(sum_x.at[h - 1, 1 - y_hi], rows_far.at[h - 1], far)])
            else:
                on_second[h] = start([
                    remote(sum_x.at[h - 1, :, target["lon"] - y_hi * nz], from_z.at[h - 1, d], target) for d, target in enumerate(z_up)
                ])

    def third(h):
        for copy in on_second[h]:
            copy.wait_recv()
        if h in far_first:
            total = sum_x[h - 1, y_hi].astype(F32) + rows_far[h - 1].astype(F32)
            sum_far[h - 1] = total.astype(BF16)
            on_last[h] = start([
                remote(sum_far.at[h - 1, target["lon"] - y_hi * nz], from_z.at[h - 1, d, 0], target) for d, target in enumerate(z_up)
            ])
            return
        if h > 0:
            total = sum_x[h - 1, :, z].astype(F32)
            for d in range(nz - 1):
                total = total + from_z[h - 1, d].astype(F32)
            sum_z[h - 1] = total.astype(BF16)
            on_last[h] = start([remote(sum_z.at[h - 1, 1 - y_hi], from_far.at[h - 1], far)])
            return
        total = first_z[:, lat].astype(F32)
        for d in range(nlat - 1):
            total = total + last_x[d].astype(F32)
        sum_y[...] = total.astype(BF16)
        on_y[h] = start([remote(sum_y.at[1 - y_hi], from_y, far)])[0]

    def last(h):
        if h == 0:
            on_y[h].wait_recv()
            total = sum_y[y_hi].astype(F32) + from_y[...].astype(F32)
        else:
            for copy in on_last[h]:
                copy.wait_recv()
            if h in far_first:
                total = sum_far[h - 1, z].astype(F32)
                for d in range(nz - 1):
                    total = total + from_z[h - 1, d, 0].astype(F32)
            else:
                total = sum_z[h - 1, y_hi].astype(F32) + from_far[h - 1].astype(F32)
        gqkv_ref[:, 192 * h : 192 * h + 192] = total[:, 0:192]
        gout_ref[:, 64 * h : 64 * h + 64] = total[:, 192:256]

    for h in (1, 0, 2, 3):
        for w in range(2):
            attend(w, h)
        if h < 3:
            weight(h)
            leave(h)

    def sum_heads(lv):
        att_l = dot(level_ref[lv], att[...]).astype(BF16)
        dqkv_l = dot(level_ref[lv], dqkv[...]).astype(BF16)
        term[lv, 0] = dot(att_l, wout_ref[...]).astype(BF16)
        term[lv, 1] = dot(dqkv_l, wqkv_ref[...], 1, 1).astype(BF16)

    chunks = [(at, CHUNK) for at in range(0, T_ROWS, CHUNK)]
    sum_heads(1 - core)
    on_core = start([
        remote(term.at[1 - core, :, pl.ds(at, size)], from_core.at[:, pl.ds(at, size)], sibling) for at, size in chunks
    ])
    weight(3)
    leave(3)
    sum_heads(core)
    onward(1)
    on_side = []
    for copy, (at, size) in zip(on_core, chunks):
        copy.wait_recv()
        rows = pl.ds(at, size)
        to_side[rows] = (term[core, 1 - kind, rows].astype(F32) + from_core[1 - kind, rows].astype(F32)).astype(BF16)
        on_side += start([remote(to_side.at[rows], from_side.at[rows], side)])
    onward(2)
    tok_l[...] = dot(level_ref[core], tokc[...])
    cot_l[...] = dot(level_ref[core], cotc[...])

    def finish(chunk):
        rows = pl.ds(*chunks[chunk])
        on_side[chunk].wait_recv()
        total = term[core, kind, rows].astype(F32) + from_core[kind, rows].astype(F32) + from_side[rows].astype(F32)

        @pl.when(kind == 0)
        def _():
            result[rows] = (tok_l[rows] + total).astype(BF16)

        @pl.when(kind == 1)
        def _():
            scaled, inverse = layer_norm(tok_l[rows])
            grad = total * gain_ref[...]
            mean_grad = jnp.mean(grad, axis=-1, keepdims=True)
            mean_mixed = jnp.mean(grad * scaled, axis=-1, keepdims=True)
            result[rows] = (cot_l[rows] + (grad - mean_grad - scaled * mean_mixed) * inverse).astype(BF16)

    def share(chunk):
        rows = pl.ds(*chunks[chunk])
        return start([
            remote(final.at[kind, core, rows], final.at[kind, core, rows], side),
            remote(final.at[kind, core, rows], final.at[kind, core, rows], sibling),
        ])

    def relay(chunk, copy):
        rows = pl.ds(*chunks[chunk])
        copy.wait_recv()
        return start([remote(final.at[1 - kind, core, rows], final.at[1 - kind, core, rows], sibling)])[0]

    def place(k, lv):
        field = dot(natural_ref[...], final[k, lv]).astype(BF16)

        @pl.when(k == 0)
        def _():
            layer_ref[lv] = field

        @pl.when(k == 1)
        def _():
            dtok_ref[lv] = field

    first, middle, end = (pl.ds(*chunk) for chunk in chunks)
    finish(0)
    straight = start([remote(result.at[first], final.at[kind, core, first], {"lat": lat_up})])[0]
    finish(1)
    spread_out[...] = dot(spread_ref[...], result[middle]).astype(BF16)
    returned = start([
        remote(spread_out.at[pl.ds(at, size)], back.at[pl.ds(at, size)], target)
        for at, size, target in ((0, 16, {"lat": lat_up}), (16, 32, {"lon": lon_up}), (48, 32, {"lat": lat_up, "lon": lon_up}))
    ])
    second(1)
    finish(2)
    onward(3)
    final[kind, core, end] = result[end]
    shared = {2: share(2)}
    straight.wait_recv()
    shared[0] = share(0)
    third(1)
    second(2)
    second(0)
    for copy in returned:
        copy.wait_recv()
    back[U_ROWS : U_ROWS + CHUNK] = result[middle]
    final[kind, core, middle] = dot(gather_ref[...], back[...]).astype(BF16)
    shared[1] = share(1)
    place(kind, core)
    relayed = [relay(2, shared[2][0]), relay(0, shared[0][0])]
    second(3)
    third(2)
    third(0)
    relayed.append(relay(1, shared[1][0]))
    third(3)
    place(1 - kind, core)
    last(1)
    for chunk in range(3):
        shared[chunk][1].wait_recv()
    place(kind, 1 - core)
    last(2)
    for copy in relayed:
        copy.wait_recv()
    place(1 - kind, 1 - core)
    last(0)
    last(3)
    for copy in started:
        copy.wait_send()


def body(tokens, norm_gain, w_qkv, w_out, bias_table, cotangent):
    nlon, nlat = lax.axis_size("lon"), lax.axis_size("lat")
    nz = nlon // 2
    width = tokens.shape[-1]
    rows = width // (nlon * nlat)
    half = CELLS // LEV
    vmem = pl.BlockSpec(memory_space=pltpu.VMEM)
    hbm = pl.BlockSpec(memory_space=pl.ANY)
    copies = 4 + 4 + (nlat - 1 + nz - 1 + 1) + 3 * (6 + nz) + 3 + 3 + 4 + 9
    shape = lambda *dims: pltpu.VMEM(dims, BF16)
    own, compact, level, spread, gather, natural, select, eye, cross = [jnp.asarray(t) for t in tables()]
    operands = (
        tokens.reshape(CELLS, width), cotangent.reshape(CELLS, width), own, bias_table.T, select, cross, compact,
        norm_gain.reshape(1, width), w_qkv, w_out, eye, level, spread, gather, natural,
    )
    layer, dtok, gqkv, gout = pl.pallas_call(
        functools.partial(kernel, nlon, nlat),
        out_shape=(shape(LEV, half, width), shape(LEV, half, width), pltpu.VMEM((rows, 768), F32), pltpu.VMEM((rows, 256), F32)),
        in_specs=[hbm] * 15,
        out_specs=(vmem,) * 4,
        scratch_shapes=[
            shape(2, G_ROWS - 112, width),
            shape(2, G_ROWS, width),
            shape(CELLS, width),
            shape(CELLS, width),
            shape(CELLS, width),
            shape(width, CELLS),
            shape(width, CELLS),
            shape(CELLS, 768),
            shape(CELLS, 256),
            pltpu.VMEM((8, 768), F32),
            pltpu.VMEM((WINDOW, SEL), F32),
            pltpu.VMEM((4, WINDOW, WINDOW), F32),
            shape(CELLS, 768),
            shape(CELLS, 256),
            shape(4, 2, nz, nlat, rows, 256),
            *[shape(3, 2, nz, rows, 128)] * 4,
            *[shape(3, 2, nz, rows, 256)] * 2,
            shape(3, 2, nz, rows, 256),
            shape(3, nz, rows, 256),
            shape(3, nz, rows, 256),
            shape(3, rows, 256),
            shape(3, 2, rows, 256),
            shape(3, max(nz - 1, 1), 2, rows, 256),
            shape(max(nz - 1, 1), 2, nlat, rows, 256),
            shape(2, nlat, rows, 256),
            shape(nlat - 1, 2, rows, 256),
            shape(2, rows, 256),
            shape(rows, 256),
            shape(LEV, 2, T_ROWS, width),
            shape(2, T_ROWS, width),
            shape(T_ROWS, width),
            shape(T_ROWS, width),
            pltpu.VMEM((T_ROWS, width), F32),
            pltpu.VMEM((T_ROWS, width), F32),
            shape(T_ROWS, width),
            shape(U_ROWS, width),
            shape(U_ROWS + CHUNK, width),
            shape(2, LEV, T_ROWS, width),
            *[pltpu.VMEM(x.shape, x.dtype) for x in operands],
            pltpu.SemaphoreType.DMA((copies,)),
            pltpu.SemaphoreType.DMA((copies,)),
            pltpu.SemaphoreType.DMA((len(operands),)),
        ],
        compiler_params=pltpu.CompilerParams(
            collective_id=0, has_side_effects=True, vmem_limit_bytes=56 * 1024 * 1024
        ),
    )(*operands)
    field = (LEV, WLAT, LON, width)
    return layer.reshape(field), dtok.reshape(field), gqkv, gout.T


def solution(mesh):
    in_specs = (
        P(None, "lat", "lon", None),
        P(),
        P(None, "head"),
        P("head", None),
        P(None, "head"),
        P(None, "lat", "lon", None),
    )
    out_specs = (
        P(None, "lat", "lon", None),
        P(None, "lat", "lon", None),
        P(("lon", "lat"), "head"),
        P("head", ("lon", "lat")),
    )
    return jax.shard_map(body, mesh=mesh, in_specs=in_specs, out_specs=out_specs, check_vma=False)
```

```python
import functools

import jax
import jax.numpy as jnp
import ml_dtypes
import numpy as np
from jax import lax
from jax.experimental import pallas as pl
from jax.experimental.pallas import tpu as pltpu
from jax.sharding import PartitionSpec as P

MESH = pl.DeviceIdType.MESH
HEAD_DIM = 64
LEV = 2
WLAT = 6
WLON = 12
LON = 24
WINDOW = LEV * WLAT * WLON
CELLS = LEV * WLAT * LON
EPSILON = 1e-05
NEG_FILL = -1e30
F32 = jnp.float32
BF16 = jnp.bfloat16

G_START = (0, 112, 224, 272)
G_ROWS = 320
T_START = (90, 0, 54, 72)
T_ROWS = 144
CHUNK = 48
U_START = (None, 0, 16, 48)
U_ROWS = 80
SEL = 384


def quarter(row, col):
    down, right = row >= 3, col >= 18
    part = (2 if right else 0) + (1 if down else 0)
    width = 6 if right else 18
    return part, (row % 3) * width + (col - 18 if right else col), 3 * width


def tables():
    own = np.zeros((G_ROWS, CELLS), np.float32)
    compact = np.zeros((CELLS, G_ROWS), np.float32)
    level = np.zeros((LEV, T_ROWS, CELLS), np.float32)
    spread = np.zeros((U_ROWS, CHUNK), np.float32)
    gather = np.zeros((CHUNK, U_ROWS + CHUNK), np.float32)
    natural = np.zeros((CELLS // LEV, T_ROWS), np.float32)
    for lv in range(LEV):
        for row in range(WLAT):
            for col in range(LON):
                part, index, size = quarter(row, col)
                held = G_START[part] + lv * size + index
                src_row = row + 3 if row < 3 else row - 3
                src_col = col + 6 if col < 18 else col - 18
                own[held, lv * 144 + src_row * LON + src_col] = 1
                place = (col // WLON) * WINDOW + lv * 72 + row * WLON + col % WLON
                compact[place, held] = 1
                level[lv, T_START[part] + index, place] = 1
                if lv == 0:
                    natural[src_row * LON + src_col, T_START[part] + index] = 1
                    at = T_START[part] + index - CHUNK
                    if 0 <= at < CHUNK and part:
                        travel = U_START[part] + (at if part == 1 else index)
                        spread[travel, at] = 1
                        gather[at, travel] = 1
                    elif 0 <= at < CHUNK:
                        gather[at, U_ROWS + at] = 1
    select = np.zeros((SEL, WINDOW), np.float32)
    for i in range(WINDOW):
        select[(i // 72) * 253 + (i // WLON % WLAT) * 23 + i % WLON, i] = 1
    half = np.arange(WINDOW) // WLON % WLAT >= 3
    cross = (half[:, None] != half[None, :]).astype(np.float32)
    exact = [t.astype(ml_dtypes.bfloat16) for t in (own, compact, level, spread, gather, natural, select, np.eye(128, dtype=np.float32))]
    return exact + [cross]


def dot(a, b, ca=1, cb=0):
    return lax.dot_general(a, b, (((ca,), (cb,)), ((), ())), preferred_element_type=F32)


def layer_norm(floats):
    center = floats - jnp.mean(floats, axis=-1, keepdims=True)
    inverse = lax.rsqrt(jnp.mean(center * center, axis=-1, keepdims=True) + EPSILON)
    return center * inverse, inverse


def kernel(
    nlon, nlat,
    tok_in, cot_in, own_in, table_in, select_in, cross_in, compact_in, gain_in, wqkv_in, wout_in, eye_in,
    level_in, spread_in, gather_in, natural_in,
    layer_ref, dtok_ref, gqkv_ref, gout_ref,
    sent, held, tokc, cotc, normed, normed_t, cot_t, qkv, datt, wide_table, rolled, bias, dqkv, att,
    wgt, relay_up, relay_down, added_up, added_down, from_below, from_above, sum_x, rows_far, sum_far, from_far, sum_z, from_z,
    near_z, first_z, last_x, sum_y, from_y,
    term, from_core, to_side, from_side, tok_l, cot_l, result, spread_out, back, final,
    tok_ref, cot_ref, own_ref, table_ref, select_ref, cross_ref, compact_ref, gain_ref, wqkv_ref, wout_ref, eye_ref,
    level_ref, spread_ref, gather_ref, natural_ref,
    send_sem, recv_sem, in_sem,
):
    lon, lat, head = lax.axis_index("lon"), lax.axis_index("lat"), lax.axis_index("head")
    nz = nlon // 2
    y_hi, z = lon // nz, lon % nz
    kind, core = head // 2, head % 2
    lat_up, lat_down = (lat + 1) % nlat, (lat + nlat - 1) % nlat
    lon_up, lon_down = (lon + 1) % nlon, (lon + nlon - 1) % nlon
    sibling = {"head": kind * 2 + 1 - core}
    side = {"head": (1 - kind) * 2 + core}
    x_up = [{"lat": (lat + d) % nlat} for d in range(1, nlat)]
    x_down = [{"lat": (lat + nlat - d) % nlat} for d in range(1, nlat)]
    z_up = [{"lon": y_hi * nz + (z + d) % nz} for d in range(1, nz)]
    z_down = [{"lon": y_hi * nz + (z + nz - d) % nz} for d in range(1, nz)]
    far = {"lon": (1 - y_hi) * nz + z}

    opposite = (lat + 2) % nlat

    sources = x_down + z_down + [
        far, sibling, side, {"lon": lon_up}, {"lon": lon_down},
        {"lat": lat_up, "lon": lon_up}, {"lat": lat_down, "lon": lon_down},
    ]
    barrier = pltpu.get_barrier_semaphore()
    for source in sources:
        pl.semaphore_signal(barrier, inc=1, device_id=source, device_id_type=MESH)

    loads = [
        pltpu.make_async_copy(src, dst, in_sem.at[i])
        for i, (src, dst) in enumerate((
            (tok_in, tok_ref), (cot_in, cot_ref), (own_in, own_ref), (table_in, table_ref), (select_in, select_ref),
            (cross_in, cross_ref), (compact_in, compact_ref), (gain_in, gain_ref), (wqkv_in, wqkv_ref), (wout_in, wout_ref),
            (eye_in, eye_ref), (level_in, level_ref), (spread_in, spread_ref), (gather_in, gather_ref), (natural_in, natural_ref),
        ))
    ]
    for load in loads:
        load.start()
    for load in loads[:3]:
        load.wait()

    count = [0]

    def remote(src, dst, target):
        index = count[0]
        count[0] += 1
        return pltpu.make_async_remote_copy(
            src_ref=src, dst_ref=dst, send_sem=send_sem.at[index], recv_sem=recv_sem.at[index],
            device_id=target, device_id_type=MESH,
        )

    started = []

    def start(copies):
        for copy in copies:
            copy.start()
        started.extend(copies)
        return copies

    for i, ref in enumerate((tok_ref, cot_ref)):
        arranged = dot(own_ref[...], ref[...]).astype(BF16)
        held[i, 0:112] = arranged[0:112]
        sent[i] = arranged[112:]
    pl.semaphore_wait(barrier, len(sources))
    diagonal = {"lat": lat_down, "lon": lon_down}
    parts = [(112, 64, {"lat": lat_down}), (224, 48, {"lon": lon_down}), (272, 48, diagonal), (176, 48, {"lat": lat_down})]
    shifted = start([
        remote(sent.at[core, pl.ds(at - 112, size)], held.at[core, pl.ds(at, size)], target) for at, size, target in parts
    ])

    for load in loads[3:]:
        load.wait()

    wide_table[...] = jnp.zeros(wide_table.shape, F32)
    wide_table[0:4, 0 : table_ref.shape[1]] = table_ref[...]
    turned = wide_table[...]
    for h in range(4):
        stepped = jnp.broadcast_to(turned[h : h + 1, :], (16, turned.shape[1]))
        stepped = pltpu.roll(stepped, 0, 1, stride=1, stride_axis=0)
        for step in range(LEV * WLAT):
            offset = (step // WLAT) * 253 + (step % WLAT) * 23
            shift = (offset - 379) % turned.shape[1]
            moved = pltpu.roll(stepped, shift, 1)
            rolled[WLON * step : WLON * step + WLON, :] = moved[0:WLON, 0:SEL]
        rest = rolled[...]
        total = jnp.zeros((WINDOW, WINDOW), F32)
        for _ in range(3):
            piece = rest.astype(BF16)
            rest = rest - piece.astype(F32)
            total = total + dot(piece, select_ref[...])
        excluded = (cross_ref[...] > 0.5) & (lat == nlat - 1)
        bias[h] = jnp.where(excluded, NEG_FILL, total)

    forwards = []
    for copy, (at, size, _) in zip(shifted, parts):
        copy.wait_recv()
        forwards += start([remote(held.at[core, pl.ds(at, size)], held.at[core, pl.ds(at, size)], sibling)])
    for copy in forwards:
        copy.wait_recv()

    tokc[...] = dot(compact_ref[...], held[0]).astype(BF16)
    cotc[...] = dot(compact_ref[...], held[1]).astype(BF16)
    for at in range(0, CELLS, 48):
        scaled, _ = layer_norm(tokc[at : at + 48, :].astype(F32))
        normed[at : at + 48, :] = (scaled * gain_ref[...]).astype(BF16)
    qkv[...] = dot(normed[...], wqkv_ref[...]).astype(BF16)
    datt[...] = dot(cotc[...], wout_ref[...], 1, 1).astype(BF16)
    for at in range(0, normed.shape[1], 128):
        normed_t[at : at + 128, :] = dot(eye_ref[...], normed[:, at : at + 128], 1, 1).astype(BF16)
        cot_t[at : at + 128, :] = dot(eye_ref[...], cotc[:, at : at + 128], 1, 1).astype(BF16)

    def attend(w, h):
        rows = pl.ds(w * WINDOW, WINDOW)
        first = 3 * HEAD_DIM * h
        query = qkv[rows, first : first + 64]
        key = qkv[rows, first + 64 : first + 128]
        value = qkv[rows, first + 128 : first + 192]
        grad = datt[rows, 64 * h : 64 * h + 64]
        scores = dot(key, query, 1, 1) * (HEAD_DIM ** -0.5) + bias[h]
        raised = jnp.exp(scores - jnp.max(scores, axis=0, keepdims=True))
        prob = raised * (1.0 / jnp.sum(raised, axis=0, keepdims=True))
        half = prob.astype(BF16)
        grad_prob = dot(value, grad, 1, 1)
        row_term = jnp.sum(prob * grad_prob, axis=0, keepdims=True)
        grad_score = (prob * (grad_prob - row_term) * (HEAD_DIM ** -0.5)).astype(BF16)
        att[rows, 64 * h : 64 * h + 64] = dot(half, value, 0, 0).astype(BF16)
        dqkv[rows, first : first + 64] = dot(grad_score, key, 0, 0).astype(BF16)
        dqkv[rows, first + 64 : first + 128] = dot(grad_score, query, 1, 0).astype(BF16)
        dqkv[rows, first + 128 : first + 192] = dot(half, grad, 1, 0).astype(BF16)

    rows_out = wgt.shape[4]
    far_first = (1,)
    on_relay, on_first, on_second, on_last, on_y = {}, {}, {}, {}, {}
    low, high = pl.ds(0, 128), pl.ds(128, 128)

    def weight(h):
        wide = dot(normed_t[...], dqkv[:, 192 * h : 192 * h + 192]).astype(BF16)
        wgt[h, :, :, :, :, 0:192] = wide.reshape(2, nz, nlat, rows_out, 192)
        narrow = dot(cot_t[...], att[:, 64 * h : 64 * h + 64]).astype(BF16)
        wgt[h, :, :, :, :, 192:256] = narrow.reshape(2, nz, nlat, rows_out, 64)

    def leave(h):
        if h == 0:
            on_first[h] = start([
                remote(wgt.at[h, :, target["lon"] - y_hi * nz], near_z.at[d], target) for d, target in enumerate(z_up)
            ])
        else:
            up, down = {"lat": lat_up}, {"lat": lat_down}
            on_relay[h] = start([
                remote(wgt.at[h, :, :, opposite, :, low], relay_up.at[h - 1], up),
                remote(wgt.at[h, :, :, opposite, :, high], relay_down.at[h - 1], down),
            ])
            on_first[h] = start([
                remote(wgt.at[h, :, :, lat_up, :, high], from_below.at[h - 1, :, :, :, high], up),
                remote(wgt.at[h, :, :, lat_down, :, low], from_above.at[h - 1, :, :, :, low], down),
            ])

    def onward(h):
        up, down = {"lat": lat_up}, {"lat": lat_down}
        for copy in on_relay[h]:
            copy.wait_recv()
        added_up[h - 1] = (wgt[h, :, :, lat_up, :, low].astype(F32) + relay_up[h - 1].astype(F32)).astype(BF16)
        added_down[h - 1] = (wgt[h, :, :, lat_down, :, high].astype(F32) + relay_down[h - 1].astype(F32)).astype(BF16)
        on_first[h] += start([
            remote(added_up.at[h - 1], from_below.at[h - 1, :, :, :, low], up),
            remote(added_down.at[h - 1], from_above.at[h - 1, :, :, :, high], down),
        ])

    def second(h):
        for copy in on_first[h]:
            copy.wait_recv()
        if h == 0:
            total = wgt[h, :, z].astype(F32)
            for d in range(nz - 1):
                total = total + near_z[d].astype(F32)
            first_z[...] = total.astype(BF16)
            on_second[h] = start([
                remote(first_z.at[:, target["lat"]], last_x.at[d], target) for d, target in enumerate(x_up)
            ])
        else:
            total = wgt[h, :, :, lat].astype(F32) + from_below[h - 1].astype(F32) + from_above[h - 1].astype(F32)
            sum_x[h - 1] = total.astype(BF16)
            if h in far_first:
                on_second[h] = start([remote(sum_x.at[h - 1, 1 - y_hi], rows_far.at[h - 1], far)])
            else:
                on_second[h] = start([
                    remote(sum_x.at[h - 1, :, target["lon"] - y_hi * nz], from_z.at[h - 1, d], target) for d, target in enumerate(z_up)
                ])

    def third(h):
        for copy in on_second[h]:
            copy.wait_recv()
        if h in far_first:
            total = sum_x[h - 1, y_hi].astype(F32) + rows_far[h - 1].astype(F32)
            sum_far[h - 1] = total.astype(BF16)
            on_last[h] = start([
                remote(sum_far.at[h - 1, target["lon"] - y_hi * nz], from_z.at[h - 1, d, 0], target) for d, target in enumerate(z_up)
            ])
            return
        if h > 0:
            total = sum_x[h - 1, :, z].astype(F32)
            for d in range(nz - 1):
                total = total + from_z[h - 1, d].astype(F32)
            sum_z[h - 1] = total.astype(BF16)
            on_last[h] = start([remote(sum_z.at[h - 1, 1 - y_hi], from_far.at[h - 1], far)])
            return
        total = first_z[:, lat].astype(F32)
        for d in range(nlat - 1):
            total = total + last_x[d].astype(F32)
        sum_y[...] = total.astype(BF16)
        on_y[h] = start([remote(sum_y.at[1 - y_hi], from_y, far)])[0]

    def last(h):
        if h == 0:
            on_y[h].wait_recv()
            total = sum_y[y_hi].astype(F32) + from_y[...].astype(F32)
        else:
            for copy in on_last[h]:
                copy.wait_recv()
            if h in far_first:
                total = sum_far[h - 1, z].astype(F32)
                for d in range(nz - 1):
                    total = total + from_z[h - 1, d, 0].astype(F32)
            else:
                total = sum_z[h - 1, y_hi].astype(F32) + from_far[h - 1].astype(F32)
        gqkv_ref[:, 192 * h : 192 * h + 192] = total[:, 0:192]
        gout_ref[:, 64 * h : 64 * h + 64] = total[:, 192:256]

    for h in (1, 0, 2, 3):
        for w in range(2):
            attend(w, h)
        if h < 3:
            weight(h)
            leave(h)

    def sum_heads(lv):
        att_l = dot(level_ref[lv], att[...]).astype(BF16)
        dqkv_l = dot(level_ref[lv], dqkv[...]).astype(BF16)
        term[lv, 0] = dot(att_l, wout_ref[...]).astype(BF16)
        term[lv, 1] = dot(dqkv_l, wqkv_ref[...], 1, 1).astype(BF16)

    chunks = [(at, CHUNK) for at in range(0, T_ROWS, CHUNK)]
    sum_heads(1 - core)
    on_core = start([
        remote(term.at[1 - core, :, pl.ds(at, size)], from_core.at[:, pl.ds(at, size)], sibling) for at, size in chunks
    ])
    weight(3)
    leave(3)
    sum_heads(core)
    onward(1)
    on_side = []
    for copy, (at, size) in zip(on_core, chunks):
        copy.wait_recv()
        rows = pl.ds(at, size)
        to_side[rows] = (term[core, 1 - kind, rows].astype(F32) + from_core[1 - kind, rows].astype(F32)).astype(BF16)
        on_side += start([remote(to_side.at[rows], from_side.at[rows], side)])
    onward(2)
    tok_l[...] = dot(level_ref[core], tokc[...])
    cot_l[...] = dot(level_ref[core], cotc[...])

    def finish(chunk):
        rows = pl.ds(*chunks[chunk])
        on_side[chunk].wait_recv()
        total = term[core, kind, rows].astype(F32) + from_core[kind, rows].astype(F32) + from_side[rows].astype(F32)

        @pl.when(kind == 0)
        def _():
            result[rows] = (tok_l[rows] + total).astype(BF16)

        @pl.when(kind == 1)
        def _():
            scaled, inverse = layer_norm(tok_l[rows])
            grad = total * gain_ref[...]
            mean_grad = jnp.mean(grad, axis=-1, keepdims=True)
            mean_mixed = jnp.mean(grad * scaled, axis=-1, keepdims=True)
            result[rows] = (cot_l[rows] + (grad - mean_grad - scaled * mean_mixed) * inverse).astype(BF16)

    def share(chunk):
        rows = pl.ds(*chunks[chunk])
        return start([
            remote(final.at[kind, core, rows], final.at[kind, core, rows], side),
            remote(final.at[kind, core, rows], final.at[kind, core, rows], sibling),
        ])

    def relay(chunk, copy):
        rows = pl.ds(*chunks[chunk])
        copy.wait_recv()
        return start([remote(final.at[1 - kind, core, rows], final.at[1 - kind, core, rows], sibling)])[0]

    def place(k, lv):
        field = dot(natural_ref[...], final[k, lv]).astype(BF16)

        @pl.when(k == 0)
        def _():
            layer_ref[lv] = field

        @pl.when(k == 1)
        def _():
            dtok_ref[lv] = field

    first, middle, end = (pl.ds(*chunk) for chunk in chunks)
    finish(0)
    straight = start([remote(result.at[first], final.at[kind, core, first], {"lat": lat_up})])[0]
    finish(1)
    spread_out[...] = dot(spread_ref[...], result[middle]).astype(BF16)
    returned = start([
        remote(spread_out.at[pl.ds(at, size)], back.at[pl.ds(at, size)], target)
        for at, size, target in ((0, 16, {"lat": lat_up}), (16, 32, {"lon": lon_up}), (48, 32, {"lat": lat_up, "lon": lon_up}))
    ])
    second(1)
    finish(2)
    onward(3)
    final[kind, core, end] = result[end]
    shared = {2: share(2)}
    straight.wait_recv()
    shared[0] = share(0)
    third(1)
    second(2)
    second(0)
    for copy in returned:
        copy.wait_recv()
    back[U_ROWS : U_ROWS + CHUNK] = result[middle]
    final[kind, core, middle] = dot(gather_ref[...], back[...]).astype(BF16)
    shared[1] = share(1)
    relayed = [relay(2, shared[2][0]), relay(0, shared[0][0])]
    second(3)
    place(kind, core)
    third(2)
    third(0)
    relayed.append(relay(1, shared[1][0]))
    third(3)
    place(1 - kind, core)
    last(1)
    for chunk in range(3):
        shared[chunk][1].wait_recv()
    place(kind, 1 - core)
    last(2)
    for copy in relayed:
        copy.wait_recv()
    place(1 - kind, 1 - core)
    last(0)
    last(3)
    for copy in started:
        copy.wait_send()


def body(tokens, norm_gain, w_qkv, w_out, bias_table, cotangent):
    nlon, nlat = lax.axis_size("lon"), lax.axis_size("lat")
    nz = nlon // 2
    width = tokens.shape[-1]
    rows = width // (nlon * nlat)
    half = CELLS // LEV
    vmem = pl.BlockSpec(memory_space=pltpu.VMEM)
    hbm = pl.BlockSpec(memory_space=pl.ANY)
    copies = 4 + 4 + (nlat - 1 + nz - 1 + 1) + 3 * (6 + nz) + 3 + 3 + 4 + 9
    shape = lambda *dims: pltpu.VMEM(dims, BF16)
    own, compact, level, spread, gather, natural, select, eye, cross = [jnp.asarray(t) for t in tables()]
    operands = (
        tokens.reshape(CELLS, width), cotangent.reshape(CELLS, width), own, bias_table.T, select, cross, compact,
        norm_gain.reshape(1, width), w_qkv, w_out, eye, level, spread, gather, natural,
    )
    layer, dtok, gqkv, gout = pl.pallas_call(
        functools.partial(kernel, nlon, nlat),
        out_shape=(shape(LEV, half, width), shape(LEV, half, width), pltpu.VMEM((rows, 768), F32), pltpu.VMEM((rows, 256), F32)),
        in_specs=[hbm] * 15,
        out_specs=(vmem,) * 4,
        scratch_shapes=[
            shape(2, G_ROWS - 112, width),
            shape(2, G_ROWS, width),
            shape(CELLS, width),
            shape(CELLS, width),
            shape(CELLS, width),
            shape(width, CELLS),
            shape(width, CELLS),
            shape(CELLS, 768),
            shape(CELLS, 256),
            pltpu.VMEM((8, 768), F32),
            pltpu.VMEM((WINDOW, SEL), F32),
            pltpu.VMEM((4, WINDOW, WINDOW), F32),
            shape(CELLS, 768),
            shape(CELLS, 256),
            shape(4, 2, nz, nlat, rows, 256),
            *[shape(3, 2, nz, rows, 128)] * 4,
            *[shape(3, 2, nz, rows, 256)] * 2,
            shape(3, 2, nz, rows, 256),
            shape(3, nz, rows, 256),
            shape(3, nz, rows, 256),
            shape(3, rows, 256),
            shape(3, 2, rows, 256),
            shape(3, max(nz - 1, 1), 2, rows, 256),
            shape(max(nz - 1, 1), 2, nlat, rows, 256),
            shape(2, nlat, rows, 256),
            shape(nlat - 1, 2, rows, 256),
            shape(2, rows, 256),
            shape(rows, 256),
            shape(LEV, 2, T_ROWS, width),
            shape(2, T_ROWS, width),
            shape(T_ROWS, width),
            shape(T_ROWS, width),
            pltpu.VMEM((T_ROWS, width), F32),
            pltpu.VMEM((T_ROWS, width), F32),
            shape(T_ROWS, width),
            shape(U_ROWS, width),
            shape(U_ROWS + CHUNK, width),
            shape(2, LEV, T_ROWS, width),
            *[pltpu.VMEM(x.shape, x.dtype) for x in operands],
            pltpu.SemaphoreType.DMA((copies,)),
            pltpu.SemaphoreType.DMA((copies,)),
            pltpu.SemaphoreType.DMA((len(operands),)),
        ],
        compiler_params=pltpu.CompilerParams(
            collective_id=0, has_side_effects=True, vmem_limit_bytes=56 * 1024 * 1024
        ),
    )(*operands)
    field = (LEV, WLAT, LON, width)
    return layer.reshape(field), dtok.reshape(field), gqkv, gout.T


def solution(mesh):
    in_specs = (
        P(None, "lat", "lon", None),
        P(),
        P(None, "head"),
        P("head", None),
        P(None, "head"),
        P(None, "lat", "lon", None),
    )
    out_specs = (
        P(None, "lat", "lon", None),
        P(None, "lat", "lon", None),
        P(("lon", "lat"), "head"),
        P("head", ("lon", "lat")),
    )
    return jax.shard_map(body, mesh=mesh, in_specs=in_specs, out_specs=out_specs, check_vma=False)
```
